32 devices in a mesh: blk: 8 (over y, x, core), ax: 4 (over z).
Axes of the slice: x: 2, y: 2, z: 4, core: 2. Of those that a mesh axis runs over, the one named last changes fastest.
Arguments:
- adjoint: bfloat16 [5, 8, 256, 64, 128], P(None, 'blk', 'ax'), may hold values from -6 to 6
- density: bfloat16 [8, 256, 64, 128], P('blk', 'ax'), may hold values from 0.5 to 1.5
- velocity: bfloat16 [3, 8, 256, 64, 128], P(None, 'blk', 'ax'), may hold values from -3 to 3
- pressure: bfloat16 [8, 256, 64, 128], P('blk', 'ax'), may hold values from 0.5 to 1.5
- metrics: bfloat16 [9, 8, 256, 64, 128], P(None, 'blk', 'ax'), may hold values from -6 to 6
- links: int32 [3, 8, 48], replicated, may hold values from -1 to 47, as said below
Outputs:
- rhs: bfloat16 [5, 8, 256, 64, 128], P(None, 'blk', 'ax')
The draws below stay inside these ranges and needn't reach their ends.
Inputs may be any that keep to these rules, and one draw needn't show every extreme that they name: links[0] is a source block or -1 (a physical boundary), links[1] a patch of that block, links[2] an orientation 0 or 1. No source patch is named twice. A block names at most 6 patches of any one source block, and some pair of blocks reaches exactly 6. The number of live patches differs between blocks, and at least one block has all 48 live.
All inputs are finite; a program needn't handle non-finite values.
Results may differ from the reference program's by a relative error of at most 0.001.
Values may be sent and summed in bfloat16 or wider, within the bound.
A program may use at most 256 MiB of HBM per device.

```python
import jax
import jax.numpy as jnp
from jax import lax

NY = 64
NZ = 128
PW = 8
NX = 256
BLOCKS = 8
PATCHES = 48
CAPACITY = 6


def draw_links(key, part):
    subkeys = jax.random.split(key, 7)
    shift_count = PATCHES // CAPACITY
    block_order = jax.random.permutation(subkeys[0], BLOCKS)
    shifts = block_order[:shift_count]
    cycle_index = jnp.arange(PATCHES, dtype=jnp.int32) % shift_count
    slot_shift = shifts[cycle_index]
    slot_face = jax.random.permutation(subkeys[1], PATCHES)
    layout = jax.random.permutation(subkeys[2], BLOCKS)
    inverse_layout = jnp.zeros((BLOCKS,), jnp.int32).at[layout].set(jnp.arange(BLOCKS, dtype=jnp.int32))
    slot_keys = jax.random.split(subkeys[3], BLOCKS)
    slot_order = jax.vmap(lambda one_key: jax.random.permutation(one_key, PATCHES))(slot_keys)
    owner_block = jnp.arange(BLOCKS, dtype=jnp.int32)[:, None]
    source = inverse_layout[(layout[owner_block] + slot_shift[slot_order]) % BLOCKS]
    source_face = slot_face[slot_order]
    live_count = jax.random.randint(subkeys[4], (BLOCKS,), PATCHES // 4, PATCHES + 1)
    full_block = jax.random.randint(subkeys[5], (), 0, BLOCKS)
    live_count = live_count.at[full_block].set(PATCHES)
    active = slot_order < live_count[:, None]
    reversed_flag = jax.random.randint(subkeys[6], (BLOCKS, PATCHES), 0, 2)
    source = jnp.where(active, source, -1)
    return jnp.stack([source, source_face, reversed_flag]).astype(jnp.int32)


def hump_profile(count, periods):
    position = (jnp.arange(count, dtype=jnp.float32) + 0.5) / count
    return jnp.sin(jnp.pi * periods * position)


def draw_adjoint(key, part):
    subkeys = jax.random.split(jax.random.fold_in(key, 917), 4)
    full_shape = (5, BLOCKS, NX, NY, NZ)
    level = jax.random.uniform(subkeys[0], (5,), jnp.float32, 3.0, 4.5)
    second_periods = 2.0
    noise = 0.1 * jax.random.truncated_normal(subkeys[2], -4.0, 4.0, full_shape, jnp.float32)
    sign_pick = jax.random.randint(subkeys[1], (5,), 0, 2)
    signed_level = level * (2.0 * sign_pick.astype(jnp.float32) - 1.0)
    second_level = jax.random.uniform(subkeys[3], (5, BLOCKS), jnp.float32, -0.5, 0.5)
    axial_main = hump_profile(NX, 1.0)
    axial_second = hump_profile(NX, second_periods)
    lateral = hump_profile(NY, 1.0)[:, None] * hump_profile(NZ, 1.0)[None, :]
    axial = signed_level[:, None, None] * axial_main[None, None, :] + second_level[:, :, None] * axial_second[None, None, :]
    smooth = axial[:, :, :, None, None] * lateral[None, None, None, :, :]
    return (smooth + noise).astype(jnp.bfloat16)


def levels(own_key, extent, cuts, low, high):
    def one(dim, parts):
        draws = jax.random.uniform(jax.random.fold_in(jax.random.fold_in(own_key, 6), dim), (parts,), jnp.float32, low / len(cuts), high / len(cuts))
        return jnp.repeat(jnp.exp(draws), extent[dim] // parts).reshape((-1,) + (1,) * (len(extent) - dim - 1))

    loudness = one(*cuts[0])
    for cut in cuts[1:]:
        loudness = loudness * one(*cut)
    return loudness


def centred(stream_key, shape, scale, bound, cuts=(), held_as=jnp.bfloat16):
    drawn = scale * jax.random.normal(stream_key, shape, jnp.float32)
    if cuts:
        drawn = drawn * levels(stream_key, shape, cuts, -0.22, 0.18)
    return jnp.clip(drawn, -bound, bound).astype(held_as)


def setup_inputs(seed: int = 0) -> dict:
    keys = jax.random.split(jax.random.key(seed), 7)
    return {
        "adjoint": draw_adjoint(jax.random.fold_in(keys[6], 71), 0),
        "density": jnp.clip(0.5 + 1.0 * jax.random.uniform(keys[1], (BLOCKS, NX, NY, NZ), jnp.float32) ** levels(keys[1], (BLOCKS, NX, NY, NZ), ((0, 8), (1, 4)), -0.2, 0.2), 0.5, 1.5).astype(jnp.bfloat16),
        "velocity": centred(keys[2], (3, BLOCKS, NX, NY, NZ), 0.5, 3.0, ((1, 8), (2, 4))),
        "pressure": jnp.clip(0.5 + 1.0 * jax.random.uniform(keys[3], (BLOCKS, NX, NY, NZ), jnp.float32) ** levels(keys[3], (BLOCKS, NX, NY, NZ), ((0, 8), (1, 4)), -0.2, 0.2), 0.5, 1.5).astype(jnp.bfloat16),
        "metrics": centred(keys[4], (9, BLOCKS, NX, NY, NZ), 1.0, 6.0, ((1, 8), (2, 4))),
        "links": draw_links(jax.random.fold_in(keys[6], 71), 0),
    }


lhs_alpha = 1.0 / 3.0
near_coef = 7.0 / 9.0
far_coef = 1.0 / 36.0
heat_ratio = 1.4
penalty_weight = 1.0

def line_tables(line_cells):
    position = jnp.arange(line_cells, dtype=jnp.int32)
    middle = jnp.ones((line_cells,), jnp.float32)
    sub_diag = jnp.where(position > 0, lhs_alpha, 0.0).astype(jnp.float32)
    super_diag = jnp.where(position < line_cells - 1, lhs_alpha, 0.0).astype(jnp.float32)
    offset = position[None, :] - position[:, None]
    stencil = near_coef * ((offset == 1).astype(jnp.float32) - (offset == -1).astype(jnp.float32))
    stencil = stencil + far_coef * ((offset == 2).astype(jnp.float32) - (offset == -2).astype(jnp.float32))
    inverse = lax.linalg.tridiagonal_solve(sub_diag, middle, super_diag, jnp.eye(line_cells, dtype=jnp.float32))
    derivative = lax.linalg.tridiagonal_solve(sub_diag, middle, super_diag, stencil)
    return (inverse, derivative)

def flux_terms(gradient, metric, density, velocity, pressure):
    contravariant = metric[0] * velocity[0] + metric[1] * velocity[1] + metric[2] * velocity[2]
    coupled = density * gradient[0] + heat_ratio * pressure * gradient[4]
    turned = (metric[0] * gradient[1] + metric[1] * gradient[2] + metric[2] * gradient[3]) / density
    return jnp.stack([contravariant * gradient[0], contravariant * gradient[1] + metric[0] * coupled, contravariant * gradient[2] + metric[1] * coupled, contravariant * gradient[3] + metric[2] * coupled, contravariant * gradient[4] + turned])

def face_patches(source_field):
    pieces = []
    for surface in (source_field[:, :, 0, :], source_field[:, :, -1, :], source_field[:, :, :, 0], source_field[:, :, :, -1]):
        fields, row_count, length = surface.shape
        grouped = surface.reshape(fields, row_count, length // PW, PW)
        pieces.append(jnp.transpose(grouped, (2, 0, 1, 3)))
    return jnp.concatenate(pieces, axis=0)

def add_patches(running, penalty):
    fields, row_count, y_count, z_count = running.shape
    z_parts = z_count // PW
    y_parts = y_count // PW

    def unfold(stacked, length):
        return jnp.transpose(stacked, (1, 2, 0, 3)).reshape(fields, row_count, length)
    running = running.at[:, :, 0, :].add(unfold(penalty[:z_parts], z_count))
    running = running.at[:, :, -1, :].add(unfold(penalty[z_parts:2 * z_parts], z_count))
    running = running.at[:, :, :, 0].add(unfold(penalty[2 * z_parts:2 * z_parts + y_parts], y_count))
    running = running.at[:, :, :, -1].add(unfold(penalty[2 * z_parts + y_parts:], y_count))
    return running

def reference(adjoint, density, velocity, pressure, metrics, links):
    highest = lax.Precision.HIGHEST
    axial_table = line_tables(NX)[1]
    cross_table = line_tables(NY)[1]
    depth_table = line_tables(NZ)[1]
    all_faces = jax.vmap(face_patches, in_axes=1)(adjoint)

    def one_block(block_id):
        block_field = lax.dynamic_index_in_dim(adjoint, block_id, 1, keepdims=False).astype(jnp.float32)
        density_f = lax.dynamic_index_in_dim(density, block_id, 0, keepdims=False).astype(jnp.float32)
        velocity_f = lax.dynamic_index_in_dim(velocity, block_id, 1, keepdims=False).astype(jnp.float32)
        pressure_f = lax.dynamic_index_in_dim(pressure, block_id, 0, keepdims=False).astype(jnp.float32)
        metric_f = lax.dynamic_index_in_dim(metrics, block_id, 1, keepdims=False).astype(jnp.float32)
        grad_x = jnp.einsum('ij,fjyz->fiyz', axial_table, block_field, precision=highest)
        grad_y = jnp.einsum('ij,fxjz->fxiz', cross_table, block_field, precision=highest)
        grad_z = jnp.einsum('ij,fxyj->fxyi', depth_table, block_field, precision=highest)
        flux_sum = flux_terms(grad_x, metric_f[0:3], density_f, velocity_f, pressure_f)
        flux_sum = flux_sum + flux_terms(grad_y, metric_f[3:6], density_f, velocity_f, pressure_f)
        flux_sum = flux_sum + flux_terms(grad_z, metric_f[6:9], density_f, velocity_f, pressure_f)
        own_faces = face_patches(block_field)
        own_links = lax.dynamic_index_in_dim(links, block_id, 1, keepdims=False)
        source = own_links[0]
        source_face = own_links[1]
        reversed_flag = own_links[2]
        neighbour = all_faces[jnp.maximum(source, 0), source_face].astype(jnp.float32)
        neighbour = jnp.where((reversed_flag == 1)[:, None, None, None], neighbour[..., ::-1], neighbour)
        penalty = jnp.where((source >= 0)[:, None, None, None], penalty_weight * (neighbour - own_faces), 0.0)
        return add_patches(flux_sum, penalty).astype(jnp.bfloat16)
    result = lax.map(one_block, jnp.arange(BLOCKS, dtype=jnp.int32))
    return jnp.transpose(result, (1, 0, 2, 3, 4))
```

```python
import functools

import jax
import jax.numpy as jnp
import numpy as np
from jax import lax
from jax.experimental import pallas as pl
from jax.experimental.pallas import tpu as pltpu
from jax.sharding import PartitionSpec as P

PW = 8
FIELDS = 5

lhs_alpha = 1.0 / 3.0
near_coef = 7.0 / 9.0
far_coef = 1.0 / 36.0
heat_ratio = 1.4
penalty_weight = 1.0

bf16 = jnp.bfloat16
f32 = jnp.float32


def tables(n):
    lhs = np.eye(n) + lhs_alpha * (np.eye(n, k=1) + np.eye(n, k=-1))
    rhs = near_coef * (np.eye(n, k=1) - np.eye(n, k=-1))
    rhs = rhs + far_coef * (np.eye(n, k=2) - np.eye(n, k=-2))
    inverse = np.linalg.inv(lhs)
    return inverse, inverse @ rhs


def split(table):
    high = table.astype(bf16)
    low = (table - high.astype(np.float64)).astype(bf16)
    return high, low


def sweep_coefs(n):
    weight = np.zeros(n)
    upper = np.zeros(n)
    for i in range(n):
        weight[i] = 1.0 / (1.0 - lhs_alpha * (upper[i - 1] if i else 0.0))
        upper[i] = lhs_alpha * weight[i]
    return weight, upper


def pack_kernel(nx, ny, nz, end_rows, target_ref, adj_ref, send_ref, ends_ref, yface, zface):
    f = pl.program_id(0)
    lane = lax.broadcasted_iota(jnp.int32, (ny, nz), 1)
    first = jnp.zeros((ny, nz), f32)
    last = jnp.zeros((ny, nz), f32)
    sides = jnp.zeros((ny, nz), f32)
    for x in range(nx):
        slab = adj_ref[0, x].astype(f32)
        first = first + float(end_rows[0, x]) * slab
        last = last + float(end_rows[1, x]) * slab
        yface[f, x : x + 1, 0:nz] = slab[0:1]
        yface[f, x : x + 1, nz : 2 * nz] = slab[ny - 1 :]
        turned = pltpu.roll(slab, 2 * x + 1, 1)
        sides = jnp.where(lane // 2 == x, turned, sides)
    ends_ref[0, 0] = first
    ends_ref[0, 1] = last
    zface[f] = sides

    @pl.when(f == FIELDS - 1)
    def _():
        row = lax.broadcasted_iota(jnp.int32, (nz, 2 * nx), 0)
        col = lax.broadcasted_iota(jnp.int32, (nz, 2 * nx), 1)
        wanted = jnp.where(col < nx, 2 * col + 1, 2 * (col - nx))
        order = jnp.where(row == wanted, 1.0, 0.0).astype(bf16)
        low, high = [], []
        for g in range(FIELDS):
            sorted_side = jnp.dot(
                zface[g].astype(bf16), order, preferred_element_type=f32
            )
            low.append(sorted_side[:, :nx])
            high.append(sorted_side[:, nx:])
        cells = jnp.concatenate(
            [jnp.concatenate(low, axis=1), jnp.concatenate(high, axis=1)], axis=0
        ).astype(bf16)
        rows = send_ref.shape[0]
        slots = lax.broadcasted_iota(jnp.int32, (rows, 2 * nz + 2 * ny), 0)
        chosen = jnp.where(slots == target_ref[...], 1.0, 0.0).astype(bf16)
        packed = lax.dot_general(
            chosen[:, : 2 * nz],
            yface[...].reshape(FIELDS * nx, 2 * nz).astype(bf16),
            (((1,), (1,)), ((), ())),
            preferred_element_type=f32,
        )
        packed = packed + jnp.dot(chosen[:, 2 * nz :], cells, preferred_element_type=f32)
        send_ref[...] = packed.astype(bf16)


def main_kernel(
    nx, ny, nz, bx,
    upper_ref, adj_ref, edge_ref, recv_ref, ysrc_ref, zsrc_ref, ymask_ref, zmask_ref,
    dy_ref, dz_ref, rho_ref, vel_ref, prs_ref, met_ref,
    out_ref,
    sweep, ypen, zpen, carry, gyz,
):
    step = pl.program_id(0)
    block = pl.num_programs(0) - 1 - step
    weight, upper = sweep_coefs(nx)
    part = 32 if ny % 32 == 0 else ny

    @pl.when(step == 0)
    def _():
        rows = recv_ref.shape[0]
        received = recv_ref[...]
        slots = lax.broadcasted_iota(jnp.int32, (rows, 2 * nz), 0)
        ypick = jnp.where(slots == ysrc_ref[...], 1.0, 0.0).astype(bf16)
        ypen[...] = lax.dot_general(
            received, ypick, (((0,), (0,)), ((), ())), preferred_element_type=f32
        ).reshape(FIELDS, nx, 2 * nz)
        slots = lax.broadcasted_iota(jnp.int32, (2 * ny, rows), 1)
        zpick = jnp.where(slots == zsrc_ref[...], 1.0, 0.0).astype(bf16)
        zcells = jnp.dot(zpick, received, preferred_element_type=f32).astype(bf16)
        row = lax.broadcasted_iota(jnp.int32, (2 * nx, nz), 0)
        col = lax.broadcasted_iota(jnp.int32, (2 * nx, nz), 1)
        wanted = jnp.where(row < nx, 2 * row + 1, 2 * (row - nx))
        order = jnp.where(col == wanted, 1.0, 0.0).astype(bf16)
        for f in range(FIELDS):
            both = jnp.concatenate(
                [zcells[:ny, f * nx : (f + 1) * nx], zcells[ny:, f * nx : (f + 1) * nx]], axis=1
            )
            zpen[f] = jnp.dot(both, order, preferred_element_type=f32)

        def forward(index, state):
            f = index // (ny // part)
            at = pl.ds(pl.multiple_of((index % (ny // part)) * part, part), part)
            zero = jnp.zeros((part, nz), f32)
            window = [zero, zero, adj_ref[f, 0, at, :].astype(f32), adj_ref[f, 1, at, :].astype(f32)]
            before = zero
            for x in range(nx):
                ahead = adj_ref[f, x + 2, at, :].astype(f32) if x + 2 < nx else zero
                window.append(ahead)
                total = near_coef * (window[3] - window[1]) + far_coef * (window[4] - window[0])
                if x < 2:
                    total = total + edge_ref[f, x, at, :]
                elif x >= nx - 2:
                    total = total + edge_ref[f, x - nx + 4, at, :]
                before = float(weight[x]) * total - float(upper[x]) * before
                sweep[f, x, at, :] = before
                window = window[1:]
            return state

        lax.fori_loop(0, FIELDS * (ny // part), forward, 0)
        carry[...] = jnp.zeros_like(carry)

    chunk = 16 if ny % 16 == 0 else ny
    unroll = 2

    def one(j, slot):
        x = block * bx + j
        slabs = [adj_ref[f, x] for f in range(FIELDS)]
        tall = jnp.concatenate(slabs, axis=0)
        gyz[slot, 0] = jnp.dot(
            jnp.concatenate([tall, tall], axis=1), dz_ref[...], preferred_element_type=f32
        ).reshape(FIELDS, ny, nz)
        wide = jnp.concatenate(slabs, axis=1)
        across = jnp.dot(
            dy_ref[...], jnp.concatenate([wide, wide], axis=0), preferred_element_type=f32
        )
        for f in range(FIELDS):
            gyz[slot, 1, f] = across[:, f * nz : (f + 1) * nz]
        back = upper_ref[x]
        group = pl.ds(pl.multiple_of(block * bx, bx), bx)
        for y0 in range(0, ny, chunk):
            at = slice(y0, y0 + chunk)
            gx = []
            for f in range(FIELDS):
                value = sweep[f, x, at, :] - back * carry[f, at, :]
                carry[f, at, :] = value
                gx.append(value)
            gy = [gyz[slot, 1, f, at, :] for f in range(FIELDS)]
            gz = [gyz[slot, 0, f, at, :] for f in range(FIELDS)]
            rho = rho_ref[j, at, :].astype(f32)
            vel = [vel_ref[c, j, at, :].astype(f32) for c in range(3)]
            prs = heat_ratio * prs_ref[j, at, :].astype(f32)
            totals = [None] * FIELDS

            def add(i, value):
                totals[i] = value if totals[i] is None else totals[i] + value

            turned = None
            for d, g in enumerate((gx, gy, gz)):
                k = [met_ref[3 * d + c, j, at, :].astype(f32) for c in range(3)]
                speed = k[0] * vel[0] + k[1] * vel[1] + k[2] * vel[2]
                coupled = rho * g[0] + prs * g[4]
                for i in range(FIELDS):
                    add(i, speed * g[i])
                for i in range(3):
                    add(i + 1, k[i] * coupled)
                dot = k[0] * g[1] + k[1] * g[2] + k[2] * g[3]
                turned = dot if turned is None else turned + dot
            add(4, turned / rho)
            zmask = zmask_ref[at, :]
            for f in range(FIELDS):
                own = adj_ref[f, x, at, :].astype(f32)
                other = pltpu.roll(zpen[f, at, :], nz - 1 - 2 * x, 1)
                total = totals[f] + zmask * (other - own)
                if y0 == 0:
                    spot = lax.broadcasted_iota(jnp.int32, (chunk, nz), 0) == 0
                    near_rows = pltpu.roll(ypen[f, group, 0:nz], lax.rem(bx - j, bx), 0)
                    jump = jnp.concatenate([near_rows] * (chunk // bx), axis=0) - own
                    total = total + jnp.where(spot, ymask_ref[0:1, :] * jump, 0.0)
                if y0 + chunk == ny:
                    spot = lax.broadcasted_iota(jnp.int32, (chunk, nz), 0) == chunk - 1
                    near_rows = pltpu.roll(ypen[f, group, nz : 2 * nz], bx - 1 - j, 0)
                    jump = jnp.concatenate([near_rows] * (chunk // bx), axis=0) - own
                    total = total + jnp.where(spot, ymask_ref[1:2, :] * jump, 0.0)
                out_ref[f, j, at, :] = total.astype(bf16)

    def several(i, state):
        for u in range(unroll):
            one(bx - 1 - (i * unroll + u), u)
        return state

    lax.fori_loop(0, bx // unroll, several, 0)


def body(adjoint, density, velocity, pressure, metrics, links):
    adj = adjoint[:, 0]
    _, nx, ny, nz = adj.shape
    blocks, patches = links.shape[1:]
    blk_count = lax.axis_size("blk")
    segments = lax.axis_size("ax")
    segment = lax.axis_index("ax")
    me = lax.axis_index("blk")
    capacity = -(-patches // blocks)
    inverse, derivative = tables(nx)

    ups = [(i, i + 1) for i in range(segments - 1)]
    downs = [(i + 1, i) for i in range(segments - 1)]
    left_halo = lax.ppermute(adj[:, nx - 2 :], "ax", ups)
    right_halo = lax.ppermute(adj[:, :2], "ax", downs)

    source, face, turn = links[0], links[1], links[2]
    earlier = np.tril(np.ones((patches, patches), bool), -1)[None]
    same = (source[:, :, None] == source[:, None, :]) & earlier
    slot = jnp.sum(same.astype(jnp.int32), axis=2)
    place = jnp.arange(blocks, dtype=jnp.int32)[:, None] * capacity + slot
    mine = (source == me)[None] & (face[None] == jnp.arange(patches, dtype=jnp.int32)[:, None, None])
    slot_of = jnp.sum(jnp.where(mine, place[None] + 1, 0), axis=(1, 2)) - 1
    cell = jnp.arange(PW, dtype=jnp.int32)[None, :]
    target = jnp.where(slot_of[:, None] >= 0, slot_of[:, None] * PW + cell, -1).reshape(1, -1)
    own_source = lax.dynamic_index_in_dim(source, me, 0, keepdims=False)[:, None]
    own_slot = lax.dynamic_index_in_dim(slot, me, 0, keepdims=False)[:, None]
    own_turn = lax.dynamic_index_in_dim(turn, me, 0, keepdims=False)[:, None]
    origin = (own_source * capacity + own_slot) * PW + jnp.where(own_turn == 1, PW - 1 - cell, cell)
    origin = jnp.where(own_source >= 0, origin, -1).reshape(1, -1)
    live = penalty_weight * jnp.broadcast_to(
        (own_source >= 0).astype(f32), (patches, PW)
    ).reshape(-1)
    ymask = live[: 2 * nz].reshape(2, nz)
    zlive = live[2 * nz :].reshape(2, ny)
    column = jnp.arange(nz, dtype=jnp.int32)[None, :]
    zmask = jnp.where(column == 0, zlive[0][:, None], 0.0)
    zmask = zmask + jnp.where(column == nz - 1, zlive[1][:, None], 0.0)

    rows = blk_count * capacity * PW
    send, ends = pl.pallas_call(
        functools.partial(pack_kernel, nx, ny, nz, derivative[[0, nx - 1]]),
        grid=(FIELDS,),
        out_shape=(
            jax.ShapeDtypeStruct((rows, FIELDS * nx), bf16),
            jax.ShapeDtypeStruct((FIELDS, 2, ny, nz), f32),
        ),
        in_specs=[
            pl.BlockSpec((1, 2 * nz + 2 * ny), lambda f: (0, 0)),
            pl.BlockSpec((1, nx, ny, nz), lambda f: (f, 0, 0, 0)),
        ],
        out_specs=(
            pl.BlockSpec((rows, FIELDS * nx), lambda f: (0, 0)),
            pl.BlockSpec((1, 2, ny, nz), lambda f: (f, 0, 0, 0)),
        ),
        scratch_shapes=[
            pltpu.VMEM((FIELDS, nx, 2 * nz), f32),
            pltpu.VMEM((FIELDS, ny, nz), f32),
        ],
        compiler_params=pltpu.CompilerParams(vmem_limit_bytes=32 << 20),
        name="pack_faces",
    )(target, adj)

    recv = lax.all_to_all(
        send.reshape(blk_count, capacity * PW, FIELDS * nx), "blk", 0, 0, tiled=True
    ).reshape(rows, FIELDS * nx)

    lo = left_halo.astype(f32)
    hi = right_halo.astype(f32)
    near, far = near_coef, far_coef
    edge = [
        -near * lo[:, 1] - far * lo[:, 0],
        -far * lo[:, 1],
        far * hi[:, 0],
        near * hi[:, 0] + far * hi[:, 1],
    ]
    spots = (0, 1, nx - 2, nx - 1)
    first_end = ends[:, 0] + sum(float(inverse[0, s]) * e for s, e in zip(spots, edge))
    last_end = ends[:, 1] + sum(float(inverse[nx - 1, s]) * e for s, e in zip(spots, edge))
    before_last = lax.ppermute(last_end.astype(bf16), "ax", ups).astype(f32)
    after_first = lax.ppermute(first_end.astype(bf16), "ax", downs).astype(f32)
    corner_first = float(inverse[0, 0])
    corner_last = float(inverse[nx - 1, nx - 1])
    shared = 1.0 - lhs_alpha * lhs_alpha * corner_first * corner_last
    left_value = jnp.where(
        segment > 0, (before_last - lhs_alpha * corner_last * first_end) / shared, 0.0
    )
    next_last = (last_end - lhs_alpha * corner_last * after_first) / shared
    right_value = jnp.where(
        segment < segments - 1, after_first - lhs_alpha * corner_first * next_last, 0.0
    )
    edge[0] = edge[0] - lhs_alpha * left_value
    edge[3] = edge[3] - lhs_alpha * right_value
    edges = jnp.stack(edge, axis=1)

    dy_high, dy_low = split(tables(ny)[1])
    dz_high, dz_low = split(tables(nz)[1])
    dy_both = jnp.asarray(np.concatenate([dy_high, dy_low], axis=1))
    dz_both = jnp.asarray(np.concatenate([dz_high.T, dz_low.T], axis=0))
    upper = jnp.asarray(sweep_coefs(nx)[1].astype(np.float32))

    bx = 8
    steps = nx // bx

    def whole(*shape):
        zeros = (0,) * len(shape)
        return pl.BlockSpec(shape, lambda i: zeros, pipeline_mode=pl.Buffered(1))

    result = pl.pallas_call(
        functools.partial(main_kernel, nx, ny, nz, bx),
        grid=(steps,),
        out_shape=jax.ShapeDtypeStruct((FIELDS, nx, ny, nz), bf16),
        in_specs=[
            pl.BlockSpec(memory_space=pltpu.SMEM),
            whole(FIELDS, nx, ny, nz),
            whole(FIELDS, 4, ny, nz),
            whole(rows, FIELDS * nx),
            whole(1, 2 * nz),
            whole(2 * ny, 1),
            whole(2, nz),
            whole(ny, nz),
            whole(ny, 2 * ny),
            whole(2 * nz, nz),
            pl.BlockSpec((bx, ny, nz), lambda i: (steps - 1 - i, 0, 0)),
            pl.BlockSpec((3, bx, ny, nz), lambda i: (0, steps - 1 - i, 0, 0)),
            pl.BlockSpec((bx, ny, nz), lambda i: (steps - 1 - i, 0, 0)),
            pl.BlockSpec((9, bx, ny, nz), lambda i: (0, steps - 1 - i, 0, 0)),
        ],
        out_specs=pl.BlockSpec((FIELDS, bx, ny, nz), lambda i: (0, steps - 1 - i, 0, 0)),
        scratch_shapes=[
            pltpu.VMEM((FIELDS, nx, ny, nz), f32),
            pltpu.VMEM((FIELDS, nx, 2 * nz), f32),
            pltpu.VMEM((FIELDS, ny, nz), f32),
            pltpu.VMEM((FIELDS, ny, nz), f32),
            pltpu.VMEM((2, 2, FIELDS, ny, nz), f32),
        ],
        compiler_params=pltpu.CompilerParams(vmem_limit_bytes=48 << 20),
        name="flux_and_penalty",
    )(
        upper, adj, edges, recv,
        origin[:, : 2 * nz], origin[:, 2 * nz :].reshape(2 * ny, 1), ymask, zmask,
        dy_both, dz_both, density[0], velocity[:, 0], pressure[0], metrics[:, 0],
    )
    return result[:, None]


def solution(mesh):
    in_specs = (
        P(None, "blk", "ax", None, None),
        P("blk", "ax", None, None),
        P(None, "blk", "ax", None, None),
        P("blk", "ax", None, None),
        P(None, "blk", "ax", None, None),
        P(),
    )
    out_specs = P(None, "blk", "ax", None, None)
    return jax.shard_map(body, mesh=mesh, in_specs=in_specs, out_specs=out_specs, check_vma=False)
```

```python
import functools

import jax
import jax.numpy as jnp
import numpy as np
from jax import lax
from jax.experimental import pallas as pl
from jax.experimental.pallas import tpu as pltpu
from jax.sharding import PartitionSpec as P

PW = 8
FIELDS = 5

lhs_alpha = 1.0 / 3.0
near_coef = 7.0 / 9.0
far_coef = 1.0 / 36.0
heat_ratio = 1.4
penalty_weight = 1.0

bf16 = jnp.bfloat16
f32 = jnp.float32


def tables(n):
    lhs = np.eye(n) + lhs_alpha * (np.eye(n, k=1) + np.eye(n, k=-1))
    rhs = near_coef * (np.eye(n, k=1) - np.eye(n, k=-1))
    rhs = rhs + far_coef * (np.eye(n, k=2) - np.eye(n, k=-2))
    inverse = np.linalg.inv(lhs)
    return inverse, inverse @ rhs


def split(table):
    high = table.astype(bf16)
    low = (table - high.astype(np.float64)).astype(bf16)
    return high, low


def sweep_coefs(n):
    weight = np.zeros(n)
    upper = np.zeros(n)
    for i in range(n):
        weight[i] = 1.0 / (1.0 - lhs_alpha * (upper[i - 1] if i else 0.0))
        upper[i] = lhs_alpha * weight[i]
    return weight, upper


def pack_kernel(
    nx, ny, nz, end_rows, target_ref, adj_ref,
    send_ref, ends_ref, yown_ref, zown_ref, yface, zface,
):
    f = pl.program_id(0)
    lane = lax.broadcasted_iota(jnp.int32, (ny, nz), 1)
    first = jnp.zeros((ny, nz), f32)
    last = jnp.zeros((ny, nz), f32)
    sides = jnp.zeros((ny, nz), f32)
    for x in range(nx):
        slab = adj_ref[0, x].astype(f32)
        first = first + float(end_rows[0, x]) * slab
        last = last + float(end_rows[1, x]) * slab
        yface[f, x : x + 1, 0:nz] = slab[0:1]
        yface[f, x : x + 1, nz : 2 * nz] = slab[ny - 1 :]
        turned = pltpu.roll(slab, 2 * x + 1, 1)
        sides = jnp.where(lane // 2 == x, turned, sides)
    ends_ref[0, 0] = first
    ends_ref[0, 1] = last
    zface[f] = sides
    zown_ref[0] = sides.astype(bf16)
    yown_ref[0] = yface[f].astype(bf16)

    @pl.when(f == FIELDS - 1)
    def _():
        row = lax.broadcasted_iota(jnp.int32, (nz, 2 * nx), 0)
        col = lax.broadcasted_iota(jnp.int32, (nz, 2 * nx), 1)
        wanted = jnp.where(col < nx, 2 * col + 1, 2 * (col - nx))
        order = jnp.where(row == wanted, 1.0, 0.0).astype(bf16)
        low, high = [], []
        for g in range(FIELDS):
            sorted_side = jnp.dot(
                zface[g].astype(bf16), order, preferred_element_type=f32
            )
            low.append(sorted_side[:, :nx])
            high.append(sorted_side[:, nx:])
        cells = jnp.concatenate(
            [jnp.concatenate(low, axis=1), jnp.concatenate(high, axis=1)], axis=0
        ).astype(bf16)
        rows = send_ref.shape[0]
        slots = lax.broadcasted_iota(jnp.int32, (rows, 2 * nz + 2 * ny), 0)
        chosen = jnp.where(slots == target_ref[...], 1.0, 0.0).astype(bf16)
        packed = lax.dot_general(
            chosen[:, : 2 * nz],
            yface[...].reshape(FIELDS * nx, 2 * nz).astype(bf16),
            (((1,), (1,)), ((), ())),
            preferred_element_type=f32,
        )
        packed = packed + jnp.dot(chosen[:, 2 * nz :], cells, preferred_element_type=f32)
        send_ref[...] = packed.astype(bf16)


def exchange_kernel(
    nx, blocks, segments, inverse,
    adj_ref, send_ref, ends_ref, recv_ref, edge_ref,
    landed, halo, ends, outgoing, beside, patch_send, patch_recv, line_send, line_recv,
):
    me = lax.axis_index("blk")
    seg = lax.axis_index("ax")
    mesh_ids = pl.DeviceIdType.MESH
    has_left = seg > 0
    has_right = seg < segments - 1

    def line_copy(number, source, target, device):
        return pltpu.make_async_remote_copy(
            src_ref=source,
            dst_ref=target,
            send_sem=line_send.at[number],
            recv_sem=line_recv.at[number],
            device_id=(me, device),
            device_id_type=mesh_ids,
        )

    halo_right = line_copy(0, adj_ref.at[:, pl.ds(nx - 2, 2)], halo.at[0], seg + 1)
    halo_left = line_copy(1, adj_ref.at[:, pl.ds(0, 2)], halo.at[1], seg - 1)
    ends_right = line_copy(2, outgoing.at[1], beside.at[0], seg + 1)
    ends_left = line_copy(3, outgoing.at[0], beside.at[1], seg - 1)

    def patch_copy(shift):
        other = lax.rem(me + shift, blocks)
        return pltpu.make_async_remote_copy(
            src_ref=send_ref.at[other],
            dst_ref=landed.at[me],
            send_sem=patch_send.at[shift],
            recv_sem=patch_recv.at[shift],
            device_id=(other, seg),
            device_id_type=mesh_ids,
        )

    barrier = pltpu.get_barrier_semaphore()
    for shift in range(1, blocks):
        pl.semaphore_signal(
            barrier, inc=1, device_id=(lax.rem(me + shift, blocks), seg), device_id_type=mesh_ids
        )

    @pl.when(has_left)
    def _():
        pl.semaphore_signal(barrier, inc=1, device_id=(me, seg - 1), device_id_type=mesh_ids)

    @pl.when(has_right)
    def _():
        pl.semaphore_signal(barrier, inc=1, device_id=(me, seg + 1), device_id_type=mesh_ids)

    @pl.when(jnp.logical_not(has_left))
    def _():
        halo[0] = jnp.zeros_like(halo[0])
        beside[0] = jnp.zeros_like(beside[0])

    @pl.when(jnp.logical_not(has_right))
    def _():
        halo[1] = jnp.zeros_like(halo[1])
        beside[1] = jnp.zeros_like(beside[1])

    pl.semaphore_wait(
        barrier, blocks - 1 + has_left.astype(jnp.int32) + has_right.astype(jnp.int32)
    )

    @pl.when(has_right)
    def _():
        halo_right.start()

    @pl.when(has_left)
    def _():
        halo_left.start()

    patches = [patch_copy(shift) for shift in range(1, blocks)]
    for copy in patches:
        copy.start()
    recv_ref[me] = send_ref[me]

    @pl.when(has_left)
    def _():
        halo_right.wait_recv()

    @pl.when(has_right)
    def _():
        halo_left.wait_recv()

    spots = (0, 1, nx - 2, nx - 1)

    def halo_terms(f):
        lo = [halo[0, f, i].astype(f32) for i in range(2)]
        hi = [halo[1, f, i].astype(f32) for i in range(2)]
        return [
            -near_coef * lo[1] - far_coef * lo[0],
            -far_coef * lo[1],
            far_coef * hi[0],
            near_coef * hi[0] + far_coef * hi[1],
        ]

    for f in range(FIELDS):
        terms = halo_terms(f)
        for side, line in ((0, 0), (1, nx - 1)):
            value = ends_ref[f, side]
            for spot, term in zip(spots, terms):
                value = value + float(inverse[line, spot]) * term
            ends[side, f] = value
            outgoing[side, f] = value.astype(bf16)

    @pl.when(has_right)
    def _():
        ends_right.start()

    @pl.when(has_left)
    def _():
        ends_left.start()

    corner_first = float(inverse[0, 0])
    corner_last = float(inverse[nx - 1, nx - 1])
    shared = 1.0 / (1.0 - lhs_alpha * lhs_alpha * corner_first * corner_last)

    @pl.when(has_left)
    def _():
        ends_right.wait_recv()

    @pl.when(has_right)
    def _():
        ends_left.wait_recv()

    for f in range(FIELDS):
        terms = halo_terms(f)
        before_last = beside[0, f].astype(f32)
        after_first = beside[1, f].astype(f32)
        left = (before_last - lhs_alpha * corner_last * ends[0, f]) * shared
        next_last = (ends[1, f] - lhs_alpha * corner_last * after_first) * shared
        right = after_first - lhs_alpha * corner_first * next_last
        edge_ref[f, 0] = terms[0] - jnp.where(has_left, lhs_alpha * left, 0.0)
        edge_ref[f, 1] = terms[1]
        edge_ref[f, 2] = terms[2]
        edge_ref[f, 3] = terms[3] - jnp.where(has_right, lhs_alpha * right, 0.0)

    for shift, copy in enumerate(patches, 1):
        copy.wait_recv()
        origin = lax.rem(me + blocks - shift, blocks)
        recv_ref[origin] = landed[origin]
    for copy in patches:
        copy.wait_send()

    @pl.when(has_right)
    def _():
        halo_right.wait_send()
        ends_right.wait_send()

    @pl.when(has_left)
    def _():
        halo_left.wait_send()
        ends_left.wait_send()


def main_kernel(
    nx, ny, nz, bx,
    upper_ref, adj_ref, edge_ref, recv_ref, ysrc_ref, zsrc_ref, ymask_ref, zmask_ref,
    yown_ref, zown_ref,
    dy_ref, dz_ref, rho_ref, vel_ref, prs_ref, met_ref,
    out_ref,
    sweep, ypen, zpen, carry, gyz,
):
    step = pl.program_id(0)
    block = pl.num_programs(0) - 1 - step
    weight, upper = sweep_coefs(nx)
    part = 32 if ny % 32 == 0 else ny

    @pl.when(step == 0)
    def _():
        rows = recv_ref.shape[0]
        received = recv_ref[...]
        slots = lax.broadcasted_iota(jnp.int32, (rows, 2 * nz), 0)
        ypick = jnp.where(slots == ysrc_ref[...], 1.0, 0.0).astype(bf16)
        yother = lax.dot_general(
            received, ypick, (((0,), (0,)), ((), ())), preferred_element_type=f32
        ).reshape(FIELDS, nx, 2 * nz)
        ypen[...] = ymask_ref[...] * (yother - yown_ref[...].astype(f32))
        slots = lax.broadcasted_iota(jnp.int32, (2 * ny, rows), 1)
        zpick = jnp.where(slots == zsrc_ref[...], 1.0, 0.0).astype(bf16)
        zcells = jnp.dot(zpick, received, preferred_element_type=f32).astype(bf16)
        row = lax.broadcasted_iota(jnp.int32, (2 * nx, nz), 0)
        col = lax.broadcasted_iota(jnp.int32, (2 * nx, nz), 1)
        wanted = jnp.where(row < nx, 2 * row + 1, 2 * (row - nx))
        order = jnp.where(col == wanted, 1.0, 0.0).astype(bf16)
        for f in range(FIELDS):
            both = jnp.concatenate(
                [zcells[:ny, f * nx : (f + 1) * nx], zcells[ny:, f * nx : (f + 1) * nx]], axis=1
            )
            zother = jnp.dot(both, order, preferred_element_type=f32)
            zpen[f] = zmask_ref[...] * (zother - zown_ref[f].astype(f32))

        def forward(index, state):
            f = index // (ny // part)
            at = pl.ds(pl.multiple_of((index % (ny // part)) * part, part), part)
            zero = jnp.zeros((part, nz), f32)
            window = [zero, zero, adj_ref[f, 0, at, :].astype(f32), adj_ref[f, 1, at, :].astype(f32)]
            before = zero
            for x in range(nx):
                ahead = adj_ref[f, x + 2, at, :].astype(f32) if x + 2 < nx else zero
                window.append(ahead)
                total = near_coef * (window[3] - window[1]) + far_coef * (window[4] - window[0])
                if x < 2:
                    total = total + edge_ref[f, x, at, :]
                elif x >= nx - 2:
                    total = total + edge_ref[f, x - nx + 4, at, :]
                before = float(weight[x]) * total - float(upper[x]) * before
                sweep[f, x, at, :] = before
                window = window[1:]
            return state

        lax.fori_loop(0, FIELDS * (ny // part), forward, 0)
        carry[...] = jnp.zeros_like(carry)

    chunk = 16 if ny % 16 == 0 else ny
    unroll = 2
    row = lax.broadcasted_iota(jnp.int32, (chunk, nz), 0)
    lane = lax.broadcasted_iota(jnp.int32, (chunk, nz), 1)
    zedge = (lane == 0) | (lane == nz - 1)

    def one(j, slot):
        x = block * bx + j
        slabs = [adj_ref[f, x] for f in range(FIELDS)]
        tall = jnp.concatenate(slabs, axis=0)
        gyz[slot, 0] = jnp.dot(
            jnp.concatenate([tall, tall], axis=1), dz_ref[...], preferred_element_type=f32
        ).reshape(FIELDS, ny, nz)
        wide = jnp.concatenate(slabs, axis=1)
        across = jnp.dot(
            dy_ref[...], jnp.concatenate([wide, wide], axis=0), preferred_element_type=f32
        )
        for f in range(FIELDS):
            gyz[slot, 1, f] = across[:, f * nz : (f + 1) * nz]
        back = upper_ref[x]
        group = pl.ds(pl.multiple_of(block * bx, bx), bx)
        for y0 in range(0, ny, chunk):
            at = slice(y0, y0 + chunk)
            gx = []
            for f in range(FIELDS):
                value = sweep[f, x, at, :] - back * carry[f, at, :]
                carry[f, at, :] = value
                gx.append(value)
            gy = [gyz[slot, 1, f, at, :] for f in range(FIELDS)]
            gz = [gyz[slot, 0, f, at, :] for f in range(FIELDS)]
            rho = rho_ref[j, at, :].astype(f32)
            vel = [vel_ref[c, j, at, :].astype(f32) for c in range(3)]
            prs = heat_ratio * prs_ref[j, at, :].astype(f32)
            totals = [None] * FIELDS

            def add(i, value):
                totals[i] = value if totals[i] is None else totals[i] + value

            turned = None
            for d, g in enumerate((gx, gy, gz)):
                k = [met_ref[3 * d + c, j, at, :].astype(f32) for c in range(3)]
                speed = k[0] * vel[0] + k[1] * vel[1] + k[2] * vel[2]
                coupled = rho * g[0] + prs * g[4]
                for i in range(FIELDS):
                    add(i, speed * g[i])
                for i in range(3):
                    add(i + 1, k[i] * coupled)
                dot = k[0] * g[1] + k[1] * g[2] + k[2] * g[3]
                turned = dot if turned is None else turned + dot
            inverse = pl.reciprocal(rho, approx=True)
            inverse = inverse * (2.0 - rho * inverse)
            add(4, turned * inverse)
            for f in range(FIELDS):
                jump = pltpu.roll(zpen[f, at, :], nz - 1 - 2 * x, 1)
                total = totals[f] + jnp.where(zedge, jump, 0.0)
                if y0 == 0:
                    jump = pltpu.roll(ypen[f, group, 0:nz], lax.rem(bx - j, bx), 0)
                    jump = jnp.concatenate([jump] * (chunk // bx), axis=0)
                    total = total + jnp.where(row == 0, jump, 0.0)
                if y0 + chunk == ny:
                    jump = pltpu.roll(ypen[f, group, nz : 2 * nz], bx - 1 - j, 0)
                    jump = jnp.concatenate([jump] * (chunk // bx), axis=0)
                    total = total + jnp.where(row == chunk - 1, jump, 0.0)
                out_ref[f, j, at, :] = total.astype(bf16)

    def several(i, state):
        for u in range(unroll):
            one(bx - 1 - (i * unroll + u), u)
        return state

    lax.fori_loop(0, bx // unroll, several, 0)


def body(adjoint, density, velocity, pressure, metrics, links):
    adj = adjoint[:, 0]
    _, nx, ny, nz = adj.shape
    blocks, patches = links.shape[1:]
    blk_count = lax.axis_size("blk")
    segments = lax.axis_size("ax")
    me = lax.axis_index("blk")
    capacity = -(-patches // blocks)
    inverse, derivative = tables(nx)

    source, face, turn = links[0], links[1], links[2]
    earlier = np.tril(np.ones((patches, patches), bool), -1)[None]
    same = (source[:, :, None] == source[:, None, :]) & earlier
    slot = jnp.sum(same.astype(jnp.int32), axis=2)
    place = jnp.arange(blocks, dtype=jnp.int32)[:, None] * capacity + slot
    mine = (source == me)[None] & (face[None] == jnp.arange(patches, dtype=jnp.int32)[:, None, None])
    slot_of = jnp.sum(jnp.where(mine, place[None] + 1, 0), axis=(1, 2)) - 1
    cell = jnp.arange(PW, dtype=jnp.int32)[None, :]
    target = jnp.where(slot_of[:, None] >= 0, slot_of[:, None] * PW + cell, -1).reshape(1, -1)
    own_source = lax.dynamic_index_in_dim(source, me, 0, keepdims=False)[:, None]
    own_slot = lax.dynamic_index_in_dim(slot, me, 0, keepdims=False)[:, None]
    own_turn = lax.dynamic_index_in_dim(turn, me, 0, keepdims=False)[:, None]
    origin = (own_source * capacity + own_slot) * PW + jnp.where(own_turn == 1, PW - 1 - cell, cell)
    origin = jnp.where(own_source >= 0, origin, -1).reshape(1, -1)
    live = penalty_weight * jnp.broadcast_to(
        (own_source >= 0).astype(f32), (patches, PW)
    ).reshape(-1)
    ymask = live[: 2 * nz].reshape(1, 2 * nz)
    zlive = live[2 * nz :].reshape(2, ny)
    column = jnp.arange(nz, dtype=jnp.int32)[None, :]
    zmask = jnp.where(column % 2 == 1, zlive[0][:, None], zlive[1][:, None])

    rows = blk_count * capacity * PW
    send, ends, yown, zown = pl.pallas_call(
        functools.partial(pack_kernel, nx, ny, nz, derivative[[0, nx - 1]]),
        grid=(FIELDS,),
        out_shape=(
            jax.ShapeDtypeStruct((rows, FIELDS * nx), bf16),
            jax.ShapeDtypeStruct((FIELDS, 2, ny, nz), f32),
            jax.ShapeDtypeStruct((FIELDS, nx, 2 * nz), bf16),
            jax.ShapeDtypeStruct((FIELDS, ny, nz), bf16),
        ),
        in_specs=[
            pl.BlockSpec((1, 2 * nz + 2 * ny), lambda f: (0, 0)),
            pl.BlockSpec((1, nx, ny, nz), lambda f: (f, 0, 0, 0)),
        ],
        out_specs=(
            pl.BlockSpec((rows, FIELDS * nx), lambda f: (0, 0)),
            pl.BlockSpec((1, 2, ny, nz), lambda f: (f, 0, 0, 0)),
            pl.BlockSpec((1, nx, 2 * nz), lambda f: (f, 0, 0)),
            pl.BlockSpec((1, ny, nz), lambda f: (f, 0, 0)),
        ),
        scratch_shapes=[
            pltpu.VMEM((FIELDS, nx, 2 * nz), f32),
            pltpu.VMEM((FIELDS, ny, nz), f32),
        ],
        compiler_params=pltpu.CompilerParams(vmem_limit_bytes=56 << 20),
        name="pack_faces",
    )(target, adj)

    slab = (capacity * PW, FIELDS * nx)
    layers = (FIELDS, 2, ny, nz)
    level = (FIELDS, ny, nz)
    vmem = pl.BlockSpec(memory_space=pltpu.VMEM)
    recv, edges = pl.pallas_call(
        functools.partial(exchange_kernel, nx, blk_count, segments, inverse),
        out_shape=(
            jax.ShapeDtypeStruct((blk_count,) + slab, bf16),
            jax.ShapeDtypeStruct((FIELDS, 4, ny, nz), f32),
        ),
        in_specs=[pl.BlockSpec(memory_space=pl.ANY), vmem, vmem],
        out_specs=(vmem, vmem),
        scratch_shapes=[
            pltpu.VMEM((blk_count,) + slab, bf16),
            pltpu.VMEM((2,) + layers, bf16),
            pltpu.VMEM((2,) + level, f32),
            pltpu.VMEM((2,) + level, bf16),
            pltpu.VMEM((2,) + level, bf16),
            pltpu.SemaphoreType.DMA((blk_count,)),
            pltpu.SemaphoreType.DMA((blk_count,)),
            pltpu.SemaphoreType.DMA((4,)),
            pltpu.SemaphoreType.DMA((4,)),
        ],
        compiler_params=pltpu.CompilerParams(
            collective_id=0, has_side_effects=True, vmem_limit_bytes=32 << 20
        ),
        name="exchange",
    )(adj, send.reshape((blk_count,) + slab), ends)
    recv = recv.reshape(rows, FIELDS * nx)

    dy_high, dy_low = split(tables(ny)[1])
    dz_high, dz_low = split(tables(nz)[1])
    dy_both = jnp.asarray(np.concatenate([dy_high, dy_low], axis=1))
    dz_both = jnp.asarray(np.concatenate([dz_high.T, dz_low.T], axis=0))
    upper = jnp.asarray(sweep_coefs(nx)[1].astype(np.float32))

    bx = 8
    steps = nx // bx

    def whole(*shape):
        zeros = (0,) * len(shape)
        return pl.BlockSpec(shape, lambda i: zeros, pipeline_mode=pl.Buffered(1))

    result = pl.pallas_call(
        functools.partial(main_kernel, nx, ny, nz, bx),
        grid=(steps,),
        out_shape=jax.ShapeDtypeStruct((FIELDS, nx, ny, nz), bf16),
        in_specs=[
            pl.BlockSpec(memory_space=pltpu.SMEM),
            whole(FIELDS, nx, ny, nz),
            whole(FIELDS, 4, ny, nz),
            whole(rows, FIELDS * nx),
            whole(1, 2 * nz),
            whole(2 * ny, 1),
            whole(1, 2 * nz),
            whole(ny, nz),
            whole(FIELDS, nx, 2 * nz),
            whole(FIELDS, ny, nz),
            whole(ny, 2 * ny),
            whole(2 * nz, nz),
            pl.BlockSpec((bx, ny, nz), lambda i: (steps - 1 - i, 0, 0)),
            pl.BlockSpec((3, bx, ny, nz), lambda i: (0, steps - 1 - i, 0, 0)),
            pl.BlockSpec((bx, ny, nz), lambda i: (steps - 1 - i, 0, 0)),
            pl.BlockSpec((9, bx, ny, nz), lambda i: (0, steps - 1 - i, 0, 0)),
        ],
        out_specs=pl.BlockSpec((FIELDS, bx, ny, nz), lambda i: (0, steps - 1 - i, 0, 0)),
        scratch_shapes=[
            pltpu.VMEM((FIELDS, nx, ny, nz), f32),
            pltpu.VMEM((FIELDS, nx, 2 * nz), f32),
            pltpu.VMEM((FIELDS, ny, nz), f32),
            pltpu.VMEM((FIELDS, ny, nz), f32),
            pltpu.VMEM((2, 2, FIELDS, ny, nz), f32),
        ],
        compiler_params=pltpu.CompilerParams(vmem_limit_bytes=48 << 20),
        name="flux_and_penalty",
    )(
        upper, adj, edges, recv,
        origin[:, : 2 * nz], origin[:, 2 * nz :].reshape(2 * ny, 1), ymask, zmask,
        yown, zown, dy_both, dz_both, density[0], velocity[:, 0], pressure[0], metrics[:, 0],
    )
    return result[:, None]


def solution(mesh):
    in_specs = (
        P(None, "blk", "ax", None, None),
        P("blk", "ax", None, None),
        P(None, "blk", "ax", None, None),
        P("blk", "ax", None, None),
        P(None, "blk", "ax", None, None),
        P(),
    )
    out_specs = P(None, "blk", "ax", None, None)
    return jax.shard_map(body, mesh=mesh, in_specs=in_specs, out_specs=out_specs, check_vma=False)
```

```python
import functools

import jax
import jax.numpy as jnp
import numpy as np
from jax import lax
from jax.experimental import pallas as pl
from jax.experimental.pallas import tpu as pltpu
from jax.sharding import PartitionSpec as P

PW = 8
FIELDS = 5

lhs_alpha = 1.0 / 3.0
near_coef = 7.0 / 9.0
far_coef = 1.0 / 36.0
heat_ratio = 1.4
penalty_weight = 1.0

bf16 = jnp.bfloat16
f32 = jnp.float32


def tables(n):
    lhs = np.eye(n) + lhs_alpha * (np.eye(n, k=1) + np.eye(n, k=-1))
    rhs = near_coef * (np.eye(n, k=1) - np.eye(n, k=-1))
    rhs = rhs + far_coef * (np.eye(n, k=2) - np.eye(n, k=-2))
    inverse = np.linalg.inv(lhs)
    return inverse, inverse @ rhs


def split(table):
    high = table.astype(bf16)
    low = (table - high.astype(np.float64)).astype(bf16)
    return high, low


def sweep_coefs(n):
    weight = np.zeros(n)
    upper = np.zeros(n)
    for i in range(n):
        weight[i] = 1.0 / (1.0 - lhs_alpha * (upper[i - 1] if i else 0.0))
        upper[i] = lhs_alpha * weight[i]
    return weight, upper


def exchange_kernel(
    nx, ny, nz, blocks, segments, inverse, end_rows,
    target_ref, adj_ref, recv_ref, edge_ref, yown_ref, zown_ref,
    fields, send_ref, yface, zface,
    landed, halo, ends, outgoing, beside,
    load_sem, patch_send, patch_recv, line_send, line_recv,
):
    def load(f):
        return pltpu.make_async_copy(adj_ref.at[f], fields.at[f], load_sem.at[f])

    for f in range(FIELDS):
        load(f).start()
    me = lax.axis_index("blk")
    seg = lax.axis_index("ax")
    mesh_ids = pl.DeviceIdType.MESH
    has_left = seg > 0
    has_right = seg < segments - 1

    def line_copy(number, source, target, device):
        return pltpu.make_async_remote_copy(
            src_ref=source,
            dst_ref=target,
            send_sem=line_send.at[number],
            recv_sem=line_recv.at[number],
            device_id=(me, device),
            device_id_type=mesh_ids,
        )

    halo_right = line_copy(0, adj_ref.at[:, pl.ds(nx - 2, 2)], halo.at[0], seg + 1)
    halo_left = line_copy(1, adj_ref.at[:, pl.ds(0, 2)], halo.at[1], seg - 1)
    ends_right = line_copy(2, outgoing.at[1], beside.at[0], seg + 1)
    ends_left = line_copy(3, outgoing.at[0], beside.at[1], seg - 1)

    def patch_copy(shift):
        other = lax.rem(me + shift, blocks)
        return pltpu.make_async_remote_copy(
            src_ref=send_ref.at[other],
            dst_ref=landed.at[me],
            send_sem=patch_send.at[shift],
            recv_sem=patch_recv.at[shift],
            device_id=(other, seg),
            device_id_type=mesh_ids,
        )

    barrier = pltpu.get_barrier_semaphore()
    for shift in range(1, blocks):
        pl.semaphore_signal(
            barrier, inc=1, device_id=(lax.rem(me + shift, blocks), seg), device_id_type=mesh_ids
        )

    @pl.when(has_left)
    def _():
        pl.semaphore_signal(barrier, inc=1, device_id=(me, seg - 1), device_id_type=mesh_ids)

    @pl.when(has_right)
    def _():
        pl.semaphore_signal(barrier, inc=1, device_id=(me, seg + 1), device_id_type=mesh_ids)

    @pl.when(jnp.logical_not(has_left))
    def _():
        halo[0] = jnp.zeros_like(halo[0])
        beside[0] = jnp.zeros_like(beside[0])

    @pl.when(jnp.logical_not(has_right))
    def _():
        halo[1] = jnp.zeros_like(halo[1])
        beside[1] = jnp.zeros_like(beside[1])

    pl.semaphore_wait(
        barrier, blocks - 1 + has_left.astype(jnp.int32) + has_right.astype(jnp.int32)
    )

    @pl.when(has_right)
    def _():
        halo_right.start()

    @pl.when(has_left)
    def _():
        halo_left.start()

    lane = lax.broadcasted_iota(jnp.int32, (ny, nz), 1)

    def read_field(f, state):
        load(f).wait()
        first = jnp.zeros((ny, nz), f32)
        last = jnp.zeros((ny, nz), f32)
        sides = jnp.zeros((ny, nz), f32)
        for x in range(nx):
            slab = fields[f, x].astype(f32)
            first = first + float(end_rows[0, x]) * slab
            last = last + float(end_rows[1, x]) * slab
            yface[f, x : x + 1, 0:nz] = slab[0:1]
            yface[f, x : x + 1, nz : 2 * nz] = slab[ny - 1 :]
            turned = pltpu.roll(slab, 2 * x + 1, 1)
            sides = jnp.where(lane // 2 == x, turned, sides)
        ends[0, f] = first
        ends[1, f] = last
        zface[f] = sides.astype(bf16)
        return state

    lax.fori_loop(0, FIELDS, read_field, 0)

    @pl.when(has_left)
    def _():
        halo_right.wait_recv()

    @pl.when(has_right)
    def _():
        halo_left.wait_recv()

    spots = (0, 1, nx - 2, nx - 1)

    def halo_terms(f):
        lo = [halo[0, f, i].astype(f32) for i in range(2)]
        hi = [halo[1, f, i].astype(f32) for i in range(2)]
        return [
            -near_coef * lo[1] - far_coef * lo[0],
            -far_coef * lo[1],
            far_coef * hi[0],
            near_coef * hi[0] + far_coef * hi[1],
        ]

    for f in range(FIELDS):
        terms = halo_terms(f)
        for side, line in ((0, 0), (1, nx - 1)):
            value = ends[side, f]
            for spot, term in zip(spots, terms):
                value = value + float(inverse[line, spot]) * term
            ends[side, f] = value
            outgoing[side, f] = value.astype(bf16)

    @pl.when(has_right)
    def _():
        ends_right.start()

    @pl.when(has_left)
    def _():
        ends_left.start()

    row = lax.broadcasted_iota(jnp.int32, (nz, 2 * nx), 0)
    col = lax.broadcasted_iota(jnp.int32, (nz, 2 * nx), 1)
    wanted = jnp.where(col < nx, 2 * col + 1, 2 * (col - nx))
    order = jnp.where(row == wanted, 1.0, 0.0).astype(bf16)
    low, high = [], []
    for f in range(FIELDS):
        sorted_side = jnp.dot(zface[f], order, preferred_element_type=f32)
        low.append(sorted_side[:, :nx])
        high.append(sorted_side[:, nx:])
    cells = jnp.concatenate(
        [jnp.concatenate(low, axis=1), jnp.concatenate(high, axis=1)], axis=0
    ).astype(bf16)
    own_rows = yface[...].astype(bf16)
    rows = blocks * send_ref.shape[1]
    slots = lax.broadcasted_iota(jnp.int32, (rows, 2 * nz + 2 * ny), 0)
    chosen = jnp.where(slots == target_ref[...], 1.0, 0.0).astype(bf16)
    packed = lax.dot_general(
        chosen[:, : 2 * nz],
        own_rows.reshape(FIELDS * nx, 2 * nz),
        (((1,), (1,)), ((), ())),
        preferred_element_type=f32,
    )
    packed = packed + jnp.dot(chosen[:, 2 * nz :], cells, preferred_element_type=f32)
    send_ref[...] = packed.astype(bf16).reshape(send_ref.shape)

    patches = [patch_copy(shift) for shift in range(1, blocks)]
    for copy in patches:
        copy.start()
    recv_ref[me] = send_ref[me]
    yown_ref[...] = own_rows
    zown_ref[...] = zface[...]

    corner_first = float(inverse[0, 0])
    corner_last = float(inverse[nx - 1, nx - 1])
    shared = 1.0 / (1.0 - lhs_alpha * lhs_alpha * corner_first * corner_last)

    @pl.when(has_left)
    def _():
        ends_right.wait_recv()

    @pl.when(has_right)
    def _():
        ends_left.wait_recv()

    for f in range(FIELDS):
        terms = halo_terms(f)
        before_last = beside[0, f].astype(f32)
        after_first = beside[1, f].astype(f32)
        left = (before_last - lhs_alpha * corner_last * ends[0, f]) * shared
        next_last = (ends[1, f] - lhs_alpha * corner_last * after_first) * shared
        right = after_first - lhs_alpha * corner_first * next_last
        edge_ref[f, 0] = terms[0] - jnp.where(has_left, lhs_alpha * left, 0.0)
        edge_ref[f, 1] = terms[1]
        edge_ref[f, 2] = terms[2]
        edge_ref[f, 3] = terms[3] - jnp.where(has_right, lhs_alpha * right, 0.0)

    for shift, copy in enumerate(patches, 1):
        copy.wait_recv()
        origin = lax.rem(me + blocks - shift, blocks)
        recv_ref[origin] = landed[origin]
    for copy in patches:
        copy.wait_send()

    @pl.when(has_right)
    def _():
        halo_right.wait_send()
        ends_right.wait_send()

    @pl.when(has_left)
    def _():
        halo_left.wait_send()
        ends_left.wait_send()


def main_kernel(
    nx, ny, nz, bx,
    upper_ref, adj_hbm, edge_ref, recv_ref, ysrc_ref, zsrc_ref, ymask_ref, zmask_ref,
    yown_ref, zown_ref,
    dy_ref, dz_ref, rho_ref, vel_ref, prs_ref, met_ref,
    out_ref,
    adj_ref, load_sem, sweep, ypen, zpen, carry, gyz,
):
    step = pl.program_id(0)
    block = pl.num_programs(0) - 1 - step
    weight, upper = sweep_coefs(nx)
    part = 32 if ny % 32 == 0 else ny

    @pl.when(step == 0)
    def _():
        half = nx // 2

        def load(f, h):
            at = pl.ds(h * half, half)
            return pltpu.make_async_copy(
                adj_hbm.at[f, at], adj_ref.at[f, at], load_sem.at[2 * f + h]
            )

        for f in range(FIELDS):
            for h in range(2):
                load(f, h).start()
        rows = recv_ref.shape[0]
        received = recv_ref[...]
        slots = lax.broadcasted_iota(jnp.int32, (rows, 2 * nz), 0)
        ypick = jnp.where(slots == ysrc_ref[...], 1.0, 0.0).astype(bf16)
        yother = lax.dot_general(
            received, ypick, (((0,), (0,)), ((), ())), preferred_element_type=f32
        ).reshape(FIELDS, nx, 2 * nz)
        ypen[...] = ymask_ref[...] * (yother - yown_ref[...].astype(f32))
        slots = lax.broadcasted_iota(jnp.int32, (2 * ny, rows), 1)
        zpick = jnp.where(slots == zsrc_ref[...], 1.0, 0.0).astype(bf16)
        zcells = jnp.dot(zpick, received, preferred_element_type=f32).astype(bf16)
        row = lax.broadcasted_iota(jnp.int32, (2 * nx, nz), 0)
        col = lax.broadcasted_iota(jnp.int32, (2 * nx, nz), 1)
        wanted = jnp.where(row < nx, 2 * row + 1, 2 * (row - nx))
        order = jnp.where(col == wanted, 1.0, 0.0).astype(bf16)
        for f in range(FIELDS):
            both = jnp.concatenate(
                [zcells[:ny, f * nx : (f + 1) * nx], zcells[ny:, f * nx : (f + 1) * nx]], axis=1
            )
            zother = jnp.dot(both, order, preferred_element_type=f32)
            zpen[f] = zmask_ref[...] * (zother - zown_ref[f].astype(f32))

        def forward(index, state):
            f = index // (ny // part)
            at = pl.ds(pl.multiple_of((index % (ny // part)) * part, part), part)

            @pl.when(index % (ny // part) == 0)
            def _():
                load(f, 0).wait()
                load(f, 1).wait()

            zero = jnp.zeros((part, nz), f32)
            window = [zero, zero, adj_ref[f, 0, at, :].astype(f32), adj_ref[f, 1, at, :].astype(f32)]
            before = zero
            for x in range(nx):
                ahead = adj_ref[f, x + 2, at, :].astype(f32) if x + 2 < nx else zero
                window.append(ahead)
                total = near_coef * (window[3] - window[1]) + far_coef * (window[4] - window[0])
                if x < 2:
                    total = total + edge_ref[f, x, at, :]
                elif x >= nx - 2:
                    total = total + edge_ref[f, x - nx + 4, at, :]
                before = float(weight[x]) * total - float(upper[x]) * before
                sweep[f, x, at, :] = before
                window = window[1:]
            return state

        lax.fori_loop(0, FIELDS * (ny // part), forward, 0)
        carry[...] = jnp.zeros_like(carry)

    chunk = 16 if ny % 16 == 0 else ny
    unroll = 2
    row = lax.broadcasted_iota(jnp.int32, (chunk, nz), 0)
    lane = lax.broadcasted_iota(jnp.int32, (chunk, nz), 1)
    zedge = (lane == 0) | (lane == nz - 1)

    def one(j, slot):
        x = block * bx + j
        slabs = [adj_ref[f, x] for f in range(FIELDS)]
        tall = jnp.concatenate(slabs, axis=0)
        gyz[slot, 0] = jnp.dot(
            jnp.concatenate([tall, tall], axis=1), dz_ref[...], preferred_element_type=f32
        ).reshape(FIELDS, ny, nz)
        wide = jnp.concatenate(slabs, axis=1)
        across = jnp.dot(
            dy_ref[...], jnp.concatenate([wide, wide], axis=0), preferred_element_type=f32
        )
        for f in range(FIELDS):
            gyz[slot, 1, f] = across[:, f * nz : (f + 1) * nz]
        back = upper_ref[x]
        group = pl.ds(pl.multiple_of(block * bx, bx), bx)
        for y0 in range(0, ny, chunk):
            at = slice(y0, y0 + chunk)
            gx = []
            for f in range(FIELDS):
                value = sweep[f, x, at, :] - back * carry[f, at, :]
                carry[f, at, :] = value
                gx.append(value)
            gy = [gyz[slot, 1, f, at, :] for f in range(FIELDS)]
            gz = [gyz[slot, 0, f, at, :] for f in range(FIELDS)]
            rho = rho_ref[j, at, :].astype(f32)
            vel = [vel_ref[c, j, at, :].astype(f32) for c in range(3)]
            prs = heat_ratio * prs_ref[j, at, :].astype(f32)
            totals = [None] * FIELDS

            def add(i, value):
                totals[i] = value if totals[i] is None else totals[i] + value

            turned = None
            for d, g in enumerate((gx, gy, gz)):
                k = [met_ref[3 * d + c, j, at, :].astype(f32) for c in range(3)]
                speed = k[0] * vel[0] + k[1] * vel[1] + k[2] * vel[2]
                coupled = rho * g[0] + prs * g[4]
                for i in range(FIELDS):
                    add(i, speed * g[i])
                for i in range(3):
                    add(i + 1, k[i] * coupled)
                dot = k[0] * g[1] + k[1] * g[2] + k[2] * g[3]
                turned = dot if turned is None else turned + dot
            inverse = pl.reciprocal(rho, approx=True)
            inverse = inverse * (2.0 - rho * inverse)
            add(4, turned * inverse)
            for f in range(FIELDS):
                jump = pltpu.roll(zpen[f, at, :], nz - 1 - 2 * x, 1)
                total = totals[f] + jnp.where(zedge, jump, 0.0)
                if y0 == 0:
                    jump = pltpu.roll(ypen[f, group, 0:nz], lax.rem(bx - j, bx), 0)
                    jump = jnp.concatenate([jump] * (chunk // bx), axis=0)
                    total = total + jnp.where(row == 0, jump, 0.0)
                if y0 + chunk == ny:
                    jump = pltpu.roll(ypen[f, group, nz : 2 * nz], bx - 1 - j, 0)
                    jump = jnp.concatenate([jump] * (chunk // bx), axis=0)
                    total = total + jnp.where(row == chunk - 1, jump, 0.0)
                out_ref[f, j, at, :] = total.astype(bf16)

    def several(i, state):
        for u in range(unroll):
            one(bx - 1 - (i * unroll + u), u)
        return state

    lax.fori_loop(0, bx // unroll, several, 0)


def body(adjoint, density, velocity, pressure, metrics, links):
    adj = adjoint[:, 0]
    _, nx, ny, nz = adj.shape
    blocks, patches = links.shape[1:]
    blk_count = lax.axis_size("blk")
    segments = lax.axis_size("ax")
    me = lax.axis_index("blk")
    capacity = -(-patches // blocks)
    inverse, derivative = tables(nx)

    source, face, turn = links[0], links[1], links[2]
    earlier = np.tril(np.ones((patches, patches), bool), -1)[None]
    same = (source[:, :, None] == source[:, None, :]) & earlier
    slot = jnp.sum(same.astype(jnp.int32), axis=2)
    place = jnp.arange(blocks, dtype=jnp.int32)[:, None] * capacity + slot
    mine = (source == me)[None] & (face[None] == jnp.arange(patches, dtype=jnp.int32)[:, None, None])
    slot_of = jnp.sum(jnp.where(mine, place[None] + 1, 0), axis=(1, 2)) - 1
    cell = jnp.arange(PW, dtype=jnp.int32)[None, :]
    target = jnp.where(slot_of[:, None] >= 0, slot_of[:, None] * PW + cell, -1).reshape(1, -1)
    own_source = lax.dynamic_index_in_dim(source, me, 0, keepdims=False)[:, None]
    own_slot = lax.dynamic_index_in_dim(slot, me, 0, keepdims=False)[:, None]
    own_turn = lax.dynamic_index_in_dim(turn, me, 0, keepdims=False)[:, None]
    origin = (own_source * capacity + own_slot) * PW + jnp.where(own_turn == 1, PW - 1 - cell, cell)
    origin = jnp.where(own_source >= 0, origin, -1).reshape(1, -1)
    live = penalty_weight * jnp.broadcast_to(
        (own_source >= 0).astype(f32), (patches, PW)
    ).reshape(-1)
    ymask = live[: 2 * nz].reshape(1, 2 * nz)
    zlive = live[2 * nz :].reshape(2, ny)
    column = jnp.arange(nz, dtype=jnp.int32)[None, :]
    zmask = jnp.where(column % 2 == 1, zlive[0][:, None], zlive[1][:, None])

    rows = blk_count * capacity * PW
    slab = (capacity * PW, FIELDS * nx)
    layers = (FIELDS, 2, ny, nz)
    level = (FIELDS, ny, nz)
    vmem = pl.BlockSpec(memory_space=pltpu.VMEM)
    recv, edges, yown, zown = pl.pallas_call(
        functools.partial(
            exchange_kernel, nx, ny, nz, blk_count, segments, inverse, derivative[[0, nx - 1]]
        ),
        out_shape=(
            jax.ShapeDtypeStruct((blk_count,) + slab, bf16),
            jax.ShapeDtypeStruct((FIELDS, 4, ny, nz), f32),
            jax.ShapeDtypeStruct((FIELDS, nx, 2 * nz), bf16),
            jax.ShapeDtypeStruct((FIELDS, ny, nz), bf16),
        ),
        in_specs=[vmem, pl.BlockSpec(memory_space=pl.ANY)],
        out_specs=(vmem, vmem, vmem, vmem),
        scratch_shapes=[
            pltpu.VMEM((FIELDS, nx, ny, nz), bf16),
            pltpu.VMEM((blk_count,) + slab, bf16),
            pltpu.VMEM((FIELDS, nx, 2 * nz), f32),
            pltpu.VMEM(level, bf16),
            pltpu.VMEM((blk_count,) + slab, bf16),
            pltpu.VMEM((2,) + layers, bf16),
            pltpu.VMEM((2,) + level, f32),
            pltpu.VMEM((2,) + level, bf16),
            pltpu.VMEM((2,) + level, bf16),
            pltpu.SemaphoreType.DMA((FIELDS,)),
            pltpu.SemaphoreType.DMA((blk_count,)),
            pltpu.SemaphoreType.DMA((blk_count,)),
            pltpu.SemaphoreType.DMA((4,)),
            pltpu.SemaphoreType.DMA((4,)),
        ],
        compiler_params=pltpu.CompilerParams(
            collective_id=0, has_side_effects=True, vmem_limit_bytes=48 << 20
        ),
        name="exchange",
    )(target, adj)
    recv = recv.reshape(rows, FIELDS * nx)

    dy_high, dy_low = split(tables(ny)[1])
    dz_high, dz_low = split(tables(nz)[1])
    dy_both = jnp.asarray(np.concatenate([dy_high, dy_low], axis=1))
    dz_both = jnp.asarray(np.concatenate([dz_high.T, dz_low.T], axis=0))
    upper = jnp.asarray(sweep_coefs(nx)[1].astype(np.float32))

    bx = 8
    steps = nx // bx

    def whole(*shape):
        zeros = (0,) * len(shape)
        return pl.BlockSpec(shape, lambda i: zeros, pipeline_mode=pl.Buffered(1))

    result = pl.pallas_call(
        functools.partial(main_kernel, nx, ny, nz, bx),
        grid=(steps,),
        out_shape=jax.ShapeDtypeStruct((FIELDS, nx, ny, nz), bf16),
        in_specs=[
            pl.BlockSpec(memory_space=pltpu.SMEM),
            pl.BlockSpec(memory_space=pl.ANY),
            whole(FIELDS, 4, ny, nz),
            whole(rows, FIELDS * nx),
            whole(1, 2 * nz),
            whole(2 * ny, 1),
            whole(1, 2 * nz),
            whole(ny, nz),
            whole(FIELDS, nx, 2 * nz),
            whole(FIELDS, ny, nz),
            whole(ny, 2 * ny),
            whole(2 * nz, nz),
            pl.BlockSpec((bx, ny, nz), lambda i: (steps - 1 - i, 0, 0)),
            pl.BlockSpec((3, bx, ny, nz), lambda i: (0, steps - 1 - i, 0, 0)),
            pl.BlockSpec((bx, ny, nz), lambda i: (steps - 1 - i, 0, 0)),
            pl.BlockSpec((9, bx, ny, nz), lambda i: (0, steps - 1 - i, 0, 0)),
        ],
        out_specs=pl.BlockSpec((FIELDS, bx, ny, nz), lambda i: (0, steps - 1 - i, 0, 0)),
        scratch_shapes=[
            pltpu.VMEM((FIELDS, nx, ny, nz), bf16),
            pltpu.SemaphoreType.DMA((2 * FIELDS,)),
            pltpu.VMEM((FIELDS, nx, ny, nz), f32),
            pltpu.VMEM((FIELDS, nx, 2 * nz), f32),
            pltpu.VMEM((FIELDS, ny, nz), f32),
            pltpu.VMEM((FIELDS, ny, nz), f32),
            pltpu.VMEM((2, 2, FIELDS, ny, nz), f32),
        ],
        compiler_params=pltpu.CompilerParams(vmem_limit_bytes=48 << 20),
        name="flux_and_penalty",
    )(
        upper, adj, edges, recv,
        origin[:, : 2 * nz], origin[:, 2 * nz :].reshape(2 * ny, 1), ymask, zmask,
        yown, zown, dy_both, dz_both, density[0], velocity[:, 0], pressure[0], metrics[:, 0],
    )
    return result[:, None]


def solution(mesh):
    in_specs = (
        P(None, "blk", "ax", None, None),
        P("blk", "ax", None, None),
        P(None, "blk", "ax", None, None),
        P("blk", "ax", None, None),
        P(None, "blk", "ax", None, None),
        P(),
    )
    out_specs = P(None, "blk", "ax", None, None)
    return jax.shard_map(body, mesh=mesh, in_specs=in_specs, out_specs=out_specs, check_vma=False)
```

```python
import functools

import jax
import jax.numpy as jnp
import numpy as np
from jax import lax
from jax.experimental import pallas as pl
from jax.experimental.pallas import tpu as pltpu
from jax.sharding import PartitionSpec as P

PW = 8
FIELDS = 5

lhs_alpha = 1.0 / 3.0
near_coef = 7.0 / 9.0
far_coef = 1.0 / 36.0
heat_ratio = 1.4
penalty_weight = 1.0

bf16 = jnp.bfloat16
f32 = jnp.float32


def tables(n):
    lhs = np.eye(n) + lhs_alpha * (np.eye(n, k=1) + np.eye(n, k=-1))
    rhs = near_coef * (np.eye(n, k=1) - np.eye(n, k=-1))
    rhs = rhs + far_coef * (np.eye(n, k=2) - np.eye(n, k=-2))
    inverse = np.linalg.inv(lhs)
    return inverse, inverse @ rhs


def split(table):
    high = table.astype(bf16)
    low = (table - high.astype(np.float64)).astype(bf16)
    return high, low


def sweep_coefs(n):
    weight = np.zeros(n)
    upper = np.zeros(n)
    for i in range(n):
        weight[i] = 1.0 / (1.0 - lhs_alpha * (upper[i - 1] if i else 0.0))
        upper[i] = lhs_alpha * weight[i]
    return weight, upper


def exchange_kernel(
    nx, ny, nz, blocks, segments, inverse, end_rows,
    links_ref, adj_ref, edge_ref, ypen_ref, zpen_ref,
    fields, send_ref, yface, zface,
    landed, halo, ends, outgoing, beside,
    load_sem, patch_send, patch_recv, line_send, line_recv,
):
    def load(f):
        return pltpu.make_async_copy(adj_ref.at[f], fields.at[f], load_sem.at[f])

    for f in range(FIELDS):
        load(f).start()
    me = lax.axis_index("blk")
    seg = lax.axis_index("ax")
    mesh_ids = pl.DeviceIdType.MESH
    has_left = seg > 0
    has_right = seg < segments - 1

    def line_copy(number, source, target, device):
        return pltpu.make_async_remote_copy(
            src_ref=source,
            dst_ref=target,
            send_sem=line_send.at[number],
            recv_sem=line_recv.at[number],
            device_id=(me, device),
            device_id_type=mesh_ids,
        )

    halo_right = line_copy(0, adj_ref.at[:, pl.ds(nx - 2, 2)], halo.at[0], seg + 1)
    halo_left = line_copy(1, adj_ref.at[:, pl.ds(0, 2)], halo.at[1], seg - 1)
    ends_right = line_copy(2, outgoing.at[1], beside.at[0], seg + 1)
    ends_left = line_copy(3, outgoing.at[0], beside.at[1], seg - 1)

    def patch_copy(shift):
        other = lax.rem(me + shift, blocks)
        return pltpu.make_async_remote_copy(
            src_ref=send_ref.at[other],
            dst_ref=landed.at[me],
            send_sem=patch_send.at[shift],
            recv_sem=patch_recv.at[shift],
            device_id=(other, seg),
            device_id_type=mesh_ids,
        )

    barrier = pltpu.get_barrier_semaphore()
    for shift in range(1, blocks):
        pl.semaphore_signal(
            barrier, inc=1, device_id=(lax.rem(me + shift, blocks), seg), device_id_type=mesh_ids
        )

    @pl.when(has_left)
    def _():
        pl.semaphore_signal(barrier, inc=1, device_id=(me, seg - 1), device_id_type=mesh_ids)

    @pl.when(has_right)
    def _():
        pl.semaphore_signal(barrier, inc=1, device_id=(me, seg + 1), device_id_type=mesh_ids)

    @pl.when(jnp.logical_not(has_left))
    def _():
        halo[0] = jnp.zeros_like(halo[0])
        beside[0] = jnp.zeros_like(beside[0])

    @pl.when(jnp.logical_not(has_right))
    def _():
        halo[1] = jnp.zeros_like(halo[1])
        beside[1] = jnp.zeros_like(beside[1])

    capacity = send_ref.shape[1] // PW
    source, face, turn = links_ref[0], links_ref[1], links_ref[2]
    patch_count = source.shape[1]
    number = lax.broadcasted_iota(jnp.int32, source.shape, 1)
    owner = lax.broadcasted_iota(jnp.int32, source.shape, 0)
    slot = jnp.zeros(source.shape, jnp.int32)
    for k in range(patch_count):
        slot = slot + jnp.where((source == source[:, k : k + 1]) & (number > k), 1, 0)
    taken = jnp.where(source == me, owner * capacity + slot + 1, 0)
    slot_of = jnp.zeros(source.shape, jnp.int32)
    for k in range(patch_count):
        slot_of = slot_of + jnp.where(face[:, k : k + 1] == number, taken[:, k : k + 1], 0)
    slot_of = jnp.sum(slot_of.astype(f32), axis=0, keepdims=True) - 1.0

    def own(values):
        return jnp.sum(jnp.where(owner == me, values, 0).astype(f32), axis=0, keepdims=True)

    own_source = own(source)
    origin_slot = jnp.where(own_source >= 0.0, own_source * capacity + own(slot), -1.0)
    live = jnp.where(own_source >= 0.0, penalty_weight, 0.0)
    facts = jnp.concatenate([slot_of, origin_slot, own(turn), live] * 2, axis=0).astype(bf16)
    cells_all = 2 * nz + 2 * ny
    spread = jnp.where(
        lax.broadcasted_iota(jnp.int32, (patch_count, cells_all), 0)
        == lax.broadcasted_iota(jnp.int32, (patch_count, cells_all), 1) // PW,
        1.0,
        0.0,
    ).astype(bf16)
    by_lane = jnp.dot(facts, spread, preferred_element_type=f32)
    spread_z = jnp.where(
        lax.broadcasted_iota(jnp.int32, (2 * ny, patch_count), 0) // PW + 2 * nz // PW
        == lax.broadcasted_iota(jnp.int32, (2 * ny, patch_count), 1),
        1.0,
        0.0,
    ).astype(bf16)
    by_row = lax.dot_general(
        spread_z, facts, (((1,), (1,)), ((), ())), preferred_element_type=f32
    )
    cell = (lax.broadcasted_iota(jnp.int32, (1, cells_all), 1) % PW).astype(f32)
    cell_z = (lax.broadcasted_iota(jnp.int32, (2 * ny, 1), 0) % PW).astype(f32)

    def spot_of(slots, turned, cells):
        return jnp.where(
            slots >= 0.0, slots * PW + jnp.where(turned > 0.5, PW - 1.0 - cells, cells), -1.0
        )

    target = spot_of(by_lane[0:1], jnp.zeros_like(cell), cell)
    yorigin = spot_of(by_lane[1:2], by_lane[2:3], cell)[:, : 2 * nz]
    zorigin = spot_of(by_row[:, 1:2], by_row[:, 2:3], cell_z)
    ylive = by_lane[3:4, : 2 * nz]
    zlive = by_row[:, 3:4]

    pl.semaphore_wait(
        barrier, blocks - 1 + has_left.astype(jnp.int32) + has_right.astype(jnp.int32)
    )

    @pl.when(has_right)
    def _():
        halo_right.start()

    @pl.when(has_left)
    def _():
        halo_left.start()

    lane = lax.broadcasted_iota(jnp.int32, (ny, nz), 1)

    def read_field(f, state):
        load(f).wait()
        first = jnp.zeros((ny, nz), f32)
        last = jnp.zeros((ny, nz), f32)
        sides = jnp.zeros((ny, nz), f32)
        for x in range(nx):
            slab = fields[f, x].astype(f32)
            first = first + float(end_rows[0, x]) * slab
            last = last + float(end_rows[1, x]) * slab
            yface[f, x : x + 1, 0:nz] = slab[0:1]
            yface[f, x : x + 1, nz : 2 * nz] = slab[ny - 1 :]
            turned = pltpu.roll(slab, 2 * x + 1, 1)
            sides = jnp.where(lane // 2 == x, turned, sides)
        ends[0, f] = first
        ends[1, f] = last
        zface[f] = sides.astype(bf16)
        return state

    lax.fori_loop(0, FIELDS, read_field, 0)

    @pl.when(has_left)
    def _():
        halo_right.wait_recv()

    @pl.when(has_right)
    def _():
        halo_left.wait_recv()

    spots = (0, 1, nx - 2, nx - 1)

    def halo_terms(f):
        lo = [halo[0, f, i].astype(f32) for i in range(2)]
        hi = [halo[1, f, i].astype(f32) for i in range(2)]
        return [
            -near_coef * lo[1] - far_coef * lo[0],
            -far_coef * lo[1],
            far_coef * hi[0],
            near_coef * hi[0] + far_coef * hi[1],
        ]

    for f in range(FIELDS):
        terms = halo_terms(f)
        for side, line in ((0, 0), (1, nx - 1)):
            value = ends[side, f]
            for spot, term in zip(spots, terms):
                value = value + float(inverse[line, spot]) * term
            ends[side, f] = value
            outgoing[side, f] = value.astype(bf16)

    @pl.when(has_right)
    def _():
        ends_right.start()

    @pl.when(has_left)
    def _():
        ends_left.start()

    row = lax.broadcasted_iota(jnp.int32, (nz, 2 * nx), 0)
    col = lax.broadcasted_iota(jnp.int32, (nz, 2 * nx), 1)
    wanted = jnp.where(col < nx, 2 * col + 1, 2 * (col - nx))
    order = jnp.where(row == wanted, 1.0, 0.0).astype(bf16)
    low, high = [], []
    for f in range(FIELDS):
        sorted_side = jnp.dot(zface[f], order, preferred_element_type=f32)
        low.append(sorted_side[:, :nx])
        high.append(sorted_side[:, nx:])
    cells = jnp.concatenate(
        [jnp.concatenate(low, axis=1), jnp.concatenate(high, axis=1)], axis=0
    ).astype(bf16)
    own_rows = yface[...].astype(bf16)
    rows = blocks * send_ref.shape[1]
    slots = lax.broadcasted_iota(jnp.int32, (rows, 2 * nz + 2 * ny), 0)
    chosen = jnp.where(slots.astype(f32) == target, 1.0, 0.0).astype(bf16)
    packed = lax.dot_general(
        chosen[:, : 2 * nz],
        own_rows.reshape(FIELDS * nx, 2 * nz),
        (((1,), (1,)), ((), ())),
        preferred_element_type=f32,
    )
    packed = packed + jnp.dot(chosen[:, 2 * nz :], cells, preferred_element_type=f32)
    send_ref[...] = packed.astype(bf16).reshape(send_ref.shape)

    patches = [patch_copy(shift) for shift in range(1, blocks)]
    for copy in patches:
        copy.start()
    landed[me] = send_ref[me]

    corner_first = float(inverse[0, 0])
    corner_last = float(inverse[nx - 1, nx - 1])
    shared = 1.0 / (1.0 - lhs_alpha * lhs_alpha * corner_first * corner_last)

    @pl.when(has_left)
    def _():
        ends_right.wait_recv()

    @pl.when(has_right)
    def _():
        ends_left.wait_recv()

    for f in range(FIELDS):
        terms = halo_terms(f)
        before_last = beside[0, f].astype(f32)
        after_first = beside[1, f].astype(f32)
        left = (before_last - lhs_alpha * corner_last * ends[0, f]) * shared
        next_last = (ends[1, f] - lhs_alpha * corner_last * after_first) * shared
        right = after_first - lhs_alpha * corner_first * next_last
        edge_ref[f, 0] = terms[0] - jnp.where(has_left, lhs_alpha * left, 0.0)
        edge_ref[f, 1] = terms[1]
        edge_ref[f, 2] = terms[2]
        edge_ref[f, 3] = terms[3] - jnp.where(has_right, lhs_alpha * right, 0.0)

    for copy in patches:
        copy.wait_recv()
    received = landed[...].reshape(rows, FIELDS * nx)
    slots = lax.broadcasted_iota(jnp.int32, (rows, 2 * nz), 0)
    ypick = jnp.where(slots.astype(f32) == yorigin, 1.0, 0.0).astype(bf16)
    yother = lax.dot_general(
        received, ypick, (((0,), (0,)), ((), ())), preferred_element_type=f32
    ).reshape(FIELDS, nx, 2 * nz)
    ypen_ref[...] = ylive * (yother - yface[...])
    slots = lax.broadcasted_iota(jnp.int32, (2 * ny, rows), 1)
    zpick = jnp.where(slots.astype(f32) == zorigin, 1.0, 0.0).astype(bf16)
    zcells = jnp.dot(zpick, received, preferred_element_type=f32).astype(bf16)
    row = lax.broadcasted_iota(jnp.int32, (2 * nx, nz), 0)
    col = lax.broadcasted_iota(jnp.int32, (2 * nx, nz), 1)
    wanted = jnp.where(row < nx, 2 * row + 1, 2 * (row - nx))
    order = jnp.where(col == wanted, 1.0, 0.0).astype(bf16)
    zmask = jnp.where(lane % 2 == 1, zlive[:ny], zlive[ny:])
    for f in range(FIELDS):
        both = jnp.concatenate(
            [zcells[:ny, f * nx : (f + 1) * nx], zcells[ny:, f * nx : (f + 1) * nx]], axis=1
        )
        zother = jnp.dot(both, order, preferred_element_type=f32)
        zpen_ref[f] = zmask * (zother - zface[f].astype(f32))
    for copy in patches:
        copy.wait_send()

    @pl.when(has_right)
    def _():
        halo_right.wait_send()
        ends_right.wait_send()

    @pl.when(has_left)
    def _():
        halo_left.wait_send()
        ends_left.wait_send()


def main_kernel(
    nx, ny, nz, bx,
    upper_ref, adj_hbm, edge_ref, ypen, zpen,
    dy_ref, dz_ref, rho_ref, vel_ref, prs_ref, met_ref,
    out_ref,
    adj_ref, load_sem, sweep, carry, gyz,
):
    step = pl.program_id(0)
    block = pl.num_programs(0) - 1 - step
    weight, upper = sweep_coefs(nx)
    part = 32 if ny % 32 == 0 else ny

    @pl.when(step == 0)
    def _():
        half = nx // 2

        def load(f, h):
            at = pl.ds(h * half, half)
            return pltpu.make_async_copy(
                adj_hbm.at[f, at], adj_ref.at[f, at], load_sem.at[2 * f + h]
            )

        for f in range(FIELDS):
            for h in range(2):
                load(f, h).start()
        def forward(index, state):
            f = index // (ny // part)
            at = pl.ds(pl.multiple_of((index % (ny // part)) * part, part), part)

            @pl.when(index % (ny // part) == 0)
            def _():
                load(f, 0).wait()
                load(f, 1).wait()

            zero = jnp.zeros((part, nz), f32)
            window = [zero, zero, adj_ref[f, 0, at, :].astype(f32), adj_ref[f, 1, at, :].astype(f32)]
            before = zero
            for x in range(nx):
                ahead = adj_ref[f, x + 2, at, :].astype(f32) if x + 2 < nx else zero
                window.append(ahead)
                total = near_coef / far_coef * (window[3] - window[1]) + (window[4] - window[0])
                scale = float(weight[x])
                if x < 2 or x >= nx - 2:
                    total = far_coef * total + edge_ref[f, x if x < 2 else x - nx + 4, at, :]
                else:
                    scale = scale * far_coef
                before = scale * total - float(upper[x]) * before
                sweep[f, x, at, :] = before
                window = window[1:]
            return state

        lax.fori_loop(0, FIELDS * (ny // part), forward, 0)
        carry[...] = jnp.zeros_like(carry)

    chunk = 16 if ny % 16 == 0 else ny
    unroll = 4
    row = lax.broadcasted_iota(jnp.int32, (chunk, nz), 0)
    lane = lax.broadcasted_iota(jnp.int32, (chunk, nz), 1)
    zedge = (lane == 0) | (lane == nz - 1)

    def one(j, slot):
        x = block * bx + j
        slabs = [adj_ref[f, x] for f in range(FIELDS)]
        tall = jnp.concatenate(slabs, axis=0)
        gyz[slot, 0] = jnp.dot(
            jnp.concatenate([tall, tall], axis=1), dz_ref[...], preferred_element_type=f32
        ).reshape(FIELDS, ny, nz)
        wide = jnp.concatenate(slabs, axis=1)
        across = jnp.dot(
            dy_ref[...], jnp.concatenate([wide, wide], axis=0), preferred_element_type=f32
        )
        for f in range(FIELDS):
            gyz[slot, 1, f] = across[:, f * nz : (f + 1) * nz]
        back = upper_ref[x]
        group = pl.ds(pl.multiple_of(block * bx, bx), bx)
        for y0 in range(0, ny, chunk):
            at = slice(y0, y0 + chunk)
            gx = []
            for f in range(FIELDS):
                value = sweep[f, x, at, :] - back * carry[f, at, :]
                carry[f, at, :] = value
                gx.append(value)
            gy = [gyz[slot, 1, f, at, :] for f in range(FIELDS)]
            gz = [gyz[slot, 0, f, at, :] for f in range(FIELDS)]
            rho = rho_ref[j, at, :].astype(f32)
            vel = [vel_ref[c, j, at, :].astype(f32) for c in range(3)]
            prs = heat_ratio * prs_ref[j, at, :].astype(f32)
            totals = [None] * FIELDS

            def add(i, value):
                totals[i] = value if totals[i] is None else totals[i] + value

            turned = None
            for d, g in enumerate((gx, gy, gz)):
                k = [met_ref[3 * d + c, j, at, :].astype(f32) for c in range(3)]
                speed = k[0] * vel[0] + k[1] * vel[1] + k[2] * vel[2]
                coupled = rho * g[0] + prs * g[4]
                for i in range(FIELDS):
                    add(i, speed * g[i])
                for i in range(3):
                    add(i + 1, k[i] * coupled)
                dot = k[0] * g[1] + k[1] * g[2] + k[2] * g[3]
                turned = dot if turned is None else turned + dot
            inverse = pl.reciprocal(rho, approx=True)
            inverse = inverse * (2.0 - rho * inverse)
            add(4, turned * inverse)
            for f in range(FIELDS):
                jump = pltpu.roll(zpen[f, at, :], nz - 1 - 2 * x, 1)
                total = totals[f] + jnp.where(zedge, jump, 0.0)
                if y0 == 0:
                    jump = pltpu.roll(ypen[f, group, 0:nz], lax.rem(bx - j, bx), 0)
                    jump = jnp.concatenate([jump] * (chunk // bx), axis=0)
                    total = total + jnp.where(row == 0, jump, 0.0)
                if y0 + chunk == ny:
                    jump = pltpu.roll(ypen[f, group, nz : 2 * nz], bx - 1 - j, 0)
                    jump = jnp.concatenate([jump] * (chunk // bx), axis=0)
                    total = total + jnp.where(row == chunk - 1, jump, 0.0)
                out_ref[f, j, at, :] = total.astype(bf16)

    def several(i, state):
        for u in range(unroll):
            one(bx - 1 - (i * unroll + u), u)
        return state

    lax.fori_loop(0, bx // unroll, several, 0)


def body(adjoint, density, velocity, pressure, metrics, links):
    adj = adjoint[:, 0]
    _, nx, ny, nz = adj.shape
    blocks, patches = links.shape[1:]
    blk_count = lax.axis_size("blk")
    segments = lax.axis_size("ax")
    capacity = -(-patches // blocks)
    inverse, derivative = tables(nx)

    slab = (capacity * PW, FIELDS * nx)
    layers = (FIELDS, 2, ny, nz)
    level = (FIELDS, ny, nz)
    vmem = pl.BlockSpec(memory_space=pltpu.VMEM)
    edges, ypen, zpen = pl.pallas_call(
        functools.partial(
            exchange_kernel, nx, ny, nz, blk_count, segments, inverse, derivative[[0, nx - 1]]
        ),
        out_shape=(
            jax.ShapeDtypeStruct((FIELDS, 4, ny, nz), f32),
            jax.ShapeDtypeStruct((FIELDS, nx, 2 * nz), f32),
            jax.ShapeDtypeStruct((FIELDS, ny, nz), f32),
        ),
        in_specs=[vmem, pl.BlockSpec(memory_space=pl.ANY)],
        out_specs=(vmem, vmem, vmem),
        scratch_shapes=[
            pltpu.VMEM((FIELDS, nx, ny, nz), bf16),
            pltpu.VMEM((blk_count,) + slab, bf16),
            pltpu.VMEM((FIELDS, nx, 2 * nz), f32),
            pltpu.VMEM(level, bf16),
            pltpu.VMEM((blk_count,) + slab, bf16),
            pltpu.VMEM((2,) + layers, bf16),
            pltpu.VMEM((2,) + level, f32),
            pltpu.VMEM((2,) + level, bf16),
            pltpu.VMEM((2,) + level, bf16),
            pltpu.SemaphoreType.DMA((FIELDS,)),
            pltpu.SemaphoreType.DMA((blk_count,)),
            pltpu.SemaphoreType.DMA((blk_count,)),
            pltpu.SemaphoreType.DMA((4,)),
            pltpu.SemaphoreType.DMA((4,)),
        ],
        compiler_params=pltpu.CompilerParams(
            collective_id=0, has_side_effects=True, vmem_limit_bytes=48 << 20
        ),
        name="exchange",
    )(links, adj)

    dy_high, dy_low = split(tables(ny)[1])
    dz_high, dz_low = split(tables(nz)[1])
    dy_both = jnp.asarray(np.concatenate([dy_high, dy_low], axis=1))
    dz_both = jnp.asarray(np.concatenate([dz_high.T, dz_low.T], axis=0))
    upper = jnp.asarray(sweep_coefs(nx)[1].astype(np.float32))

    bx = 8
    steps = nx // bx

    def whole(*shape):
        zeros = (0,) * len(shape)
        return pl.BlockSpec(shape, lambda i: zeros, pipeline_mode=pl.Buffered(1))

    result = pl.pallas_call(
        functools.partial(main_kernel, nx, ny, nz, bx),
        grid=(steps,),
        out_shape=jax.ShapeDtypeStruct((FIELDS, nx, ny, nz), bf16),
        in_specs=[
            pl.BlockSpec(memory_space=pltpu.SMEM),
            pl.BlockSpec(memory_space=pl.ANY),
            whole(FIELDS, 4, ny, nz),
            whole(FIELDS, nx, 2 * nz),
            whole(FIELDS, ny, nz),
            whole(ny, 2 * ny),
            whole(2 * nz, nz),
            pl.BlockSpec((bx, ny, nz), lambda i: (steps - 1 - i, 0, 0)),
            pl.BlockSpec((3, bx, ny, nz), lambda i: (0, steps - 1 - i, 0, 0)),
            pl.BlockSpec((bx, ny, nz), lambda i: (steps - 1 - i, 0, 0)),
            pl.BlockSpec((9, bx, ny, nz), lambda i: (0, steps - 1 - i, 0, 0)),
        ],
        out_specs=pl.BlockSpec((FIELDS, bx, ny, nz), lambda i: (0, steps - 1 - i, 0, 0)),
        scratch_shapes=[
            pltpu.VMEM((FIELDS, nx, ny, nz), bf16),
            pltpu.SemaphoreType.DMA((2 * FIELDS,)),
            pltpu.VMEM((FIELDS, nx, ny, nz), f32),
            pltpu.VMEM((FIELDS, ny, nz), f32),
            pltpu.VMEM((4, 2, FIELDS, ny, nz), f32),
        ],
        compiler_params=pltpu.CompilerParams(vmem_limit_bytes=48 << 20),
        name="flux_and_penalty",
    )(
        upper, adj, edges, ypen, zpen, dy_both, dz_both,
        density[0], velocity[:, 0], pressure[0], metrics[:, 0],
    )
    return result[:, None]


def solution(mesh):
    in_specs = (
        P(None, "blk", "ax", None, None),
        P("blk", "ax", None, None),
        P(None, "blk", "ax", None, None),
        P("blk", "ax", None, None),
        P(None, "blk", "ax", None, None),
        P(),
    )
    out_specs = P(None, "blk", "ax", None, None)
    return jax.shard_map(body, mesh=mesh, in_specs=in_specs, out_specs=out_specs, check_vma=False)
```

```python
import functools

import jax
import jax.numpy as jnp
import numpy as np
from jax import lax
from jax.experimental import pallas as pl
from jax.experimental.pallas import tpu as pltpu
from jax.sharding import PartitionSpec as P

PW = 8
FIELDS = 5

lhs_alpha = 1.0 / 3.0
near_coef = 7.0 / 9.0
far_coef = 1.0 / 36.0
heat_ratio = 1.4
penalty_weight = 1.0

bf16 = jnp.bfloat16
f32 = jnp.float32


def tables(n):
    lhs = np.eye(n) + lhs_alpha * (np.eye(n, k=1) + np.eye(n, k=-1))
    rhs = near_coef * (np.eye(n, k=1) - np.eye(n, k=-1))
    rhs = rhs + far_coef * (np.eye(n, k=2) - np.eye(n, k=-2))
    inverse = np.linalg.inv(lhs)
    return inverse, inverse @ rhs


def split(table):
    high = table.astype(bf16)
    low = (table - high.astype(np.float64)).astype(bf16)
    return high, low


def sweep_coefs(n):
    weight = np.zeros(n)
    upper = np.zeros(n)
    for i in range(n):
        weight[i] = 1.0 / (1.0 - lhs_alpha * (upper[i - 1] if i else 0.0))
        upper[i] = lhs_alpha * weight[i]
    return weight, upper


def exchange_kernel(
    nx, ny, nz, blocks, segments, inverse, end_rows,
    links_ref, adj_ref, edge_ref, ypen_ref, zpen_ref,
    fields, send_ref, yface, zface,
    landed, halo, ends, outgoing, beside,
    load_sem, patch_send, patch_recv, line_send, line_recv,
):
    def load(f):
        return pltpu.make_async_copy(adj_ref.at[f], fields.at[f], load_sem.at[f])

    for f in range(FIELDS):
        load(f).start()
    me = lax.axis_index("blk")
    seg = lax.axis_index("ax")
    mesh_ids = pl.DeviceIdType.MESH
    has_left = seg > 0
    has_right = seg < segments - 1

    def line_copy(number, source, target, device):
        return pltpu.make_async_remote_copy(
            src_ref=source,
            dst_ref=target,
            send_sem=line_send.at[number],
            recv_sem=line_recv.at[number],
            device_id=(me, device),
            device_id_type=mesh_ids,
        )

    halo_right = line_copy(0, adj_ref.at[:, pl.ds(nx - 2, 2)], halo.at[0], seg + 1)
    halo_left = line_copy(1, adj_ref.at[:, pl.ds(0, 2)], halo.at[1], seg - 1)
    ends_right = line_copy(2, outgoing.at[1], beside.at[0], seg + 1)
    ends_left = line_copy(3, outgoing.at[0], beside.at[1], seg - 1)

    def patch_copy(shift):
        other = lax.rem(me + shift, blocks)
        return pltpu.make_async_remote_copy(
            src_ref=send_ref.at[other],
            dst_ref=landed.at[me],
            send_sem=patch_send.at[shift],
            recv_sem=patch_recv.at[shift],
            device_id=(other, seg),
            device_id_type=mesh_ids,
        )

    barrier = pltpu.get_barrier_semaphore()
    for shift in range(1, blocks):
        pl.semaphore_signal(
            barrier, inc=1, device_id=(lax.rem(me + shift, blocks), seg), device_id_type=mesh_ids
        )

    @pl.when(has_left)
    def _():
        pl.semaphore_signal(barrier, inc=1, device_id=(me, seg - 1), device_id_type=mesh_ids)

    @pl.when(has_right)
    def _():
        pl.semaphore_signal(barrier, inc=1, device_id=(me, seg + 1), device_id_type=mesh_ids)

    @pl.when(jnp.logical_not(has_left))
    def _():
        halo[0] = jnp.zeros_like(halo[0])
        beside[0] = jnp.zeros_like(beside[0])

    @pl.when(jnp.logical_not(has_right))
    def _():
        halo[1] = jnp.zeros_like(halo[1])
        beside[1] = jnp.zeros_like(beside[1])

    capacity = send_ref.shape[1] // PW
    source, face, turn = links_ref[0], links_ref[1], links_ref[2]
    patch_count = source.shape[1]
    number = lax.broadcasted_iota(jnp.int32, source.shape, 1)
    owner = lax.broadcasted_iota(jnp.int32, source.shape, 0)
    slot = jnp.zeros(source.shape, jnp.int32)
    for k in range(patch_count):
        slot = slot + jnp.where((source == source[:, k : k + 1]) & (number > k), 1, 0)
    taken = jnp.where(source == me, owner * capacity + slot + 1, 0)
    slot_of = jnp.zeros(source.shape, jnp.int32)
    for k in range(patch_count):
        slot_of = slot_of + jnp.where(face[:, k : k + 1] == number, taken[:, k : k + 1], 0)
    slot_of = jnp.sum(slot_of.astype(f32), axis=0, keepdims=True) - 1.0

    def own(values):
        return jnp.sum(jnp.where(owner == me, values, 0).astype(f32), axis=0, keepdims=True)

    own_source = own(source)
    origin_slot = jnp.where(own_source >= 0.0, own_source * capacity + own(slot), -1.0)
    live = jnp.where(own_source >= 0.0, penalty_weight, 0.0)
    facts = jnp.concatenate([slot_of, origin_slot, own(turn), live] * 2, axis=0).astype(bf16)
    cells_all = 2 * nz + 2 * ny
    spread = jnp.where(
        lax.broadcasted_iota(jnp.int32, (patch_count, cells_all), 0)
        == lax.broadcasted_iota(jnp.int32, (patch_count, cells_all), 1) // PW,
        1.0,
        0.0,
    ).astype(bf16)
    by_lane = jnp.dot(facts, spread, preferred_element_type=f32)
    spread_z = jnp.where(
        lax.broadcasted_iota(jnp.int32, (2 * ny, patch_count), 0) // PW + 2 * nz // PW
        == lax.broadcasted_iota(jnp.int32, (2 * ny, patch_count), 1),
        1.0,
        0.0,
    ).astype(bf16)
    by_row = lax.dot_general(
        spread_z, facts, (((1,), (1,)), ((), ())), preferred_element_type=f32
    )
    cell = (lax.broadcasted_iota(jnp.int32, (1, cells_all), 1) % PW).astype(f32)
    cell_z = (lax.broadcasted_iota(jnp.int32, (2 * ny, 1), 0) % PW).astype(f32)

    def spot_of(slots, turned, cells):
        return jnp.where(
            slots >= 0.0, slots * PW + jnp.where(turned > 0.5, PW - 1.0 - cells, cells), -1.0
        )

    target = spot_of(by_lane[0:1], jnp.zeros_like(cell), cell)
    yorigin = spot_of(by_lane[1:2], by_lane[2:3], cell)[:, : 2 * nz]
    zorigin = spot_of(by_row[:, 1:2], by_row[:, 2:3], cell_z)
    ylive = by_lane[3:4, : 2 * nz]
    zlive = by_row[:, 3:4]

    pl.semaphore_wait(
        barrier, blocks - 1 + has_left.astype(jnp.int32) + has_right.astype(jnp.int32)
    )

    @pl.when(has_right)
    def _():
        halo_right.start()

    @pl.when(has_left)
    def _():
        halo_left.start()

    lane = lax.broadcasted_iota(jnp.int32, (ny, nz), 1)

    def read_field(f, state):
        load(f).wait()
        first = jnp.zeros((ny, nz), f32)
        last = jnp.zeros((ny, nz), f32)
        sides = jnp.zeros((ny, nz), f32)
        for x in range(nx):
            slab = fields[f, x].astype(f32)
            first = first + float(end_rows[0, x]) * slab
            last = last + float(end_rows[1, x]) * slab
            yface[f, x : x + 1, 0:nz] = slab[0:1]
            yface[f, x : x + 1, nz : 2 * nz] = slab[ny - 1 :]
            turned = pltpu.roll(slab, 2 * x + 1, 1)
            sides = jnp.where(lane // 2 == x, turned, sides)
        ends[0, f] = first
        ends[1, f] = last
        zface[f] = sides.astype(bf16)
        return state

    lax.fori_loop(0, FIELDS, read_field, 0)

    @pl.when(has_left)
    def _():
        halo_right.wait_recv()

    @pl.when(has_right)
    def _():
        halo_left.wait_recv()

    spots = (0, 1, nx - 2, nx - 1)

    def halo_terms(f):
        lo = [halo[0, f, i].astype(f32) for i in range(2)]
        hi = [halo[1, f, i].astype(f32) for i in range(2)]
        return [
            -near_coef * lo[1] - far_coef * lo[0],
            -far_coef * lo[1],
            far_coef * hi[0],
            near_coef * hi[0] + far_coef * hi[1],
        ]

    for f in range(FIELDS):
        terms = halo_terms(f)
        for side, line in ((0, 0), (1, nx - 1)):
            value = ends[side, f]
            for spot, term in zip(spots, terms):
                value = value + float(inverse[line, spot]) * term
            ends[side, f] = value
            outgoing[side, f] = value.astype(bf16)

    @pl.when(has_right)
    def _():
        ends_right.start()

    @pl.when(has_left)
    def _():
        ends_left.start()

    row = lax.broadcasted_iota(jnp.int32, (nz, 2 * nx), 0)
    col = lax.broadcasted_iota(jnp.int32, (nz, 2 * nx), 1)
    wanted = jnp.where(col < nx, 2 * col + 1, 2 * (col - nx))
    order = jnp.where(row == wanted, 1.0, 0.0).astype(bf16)
    low, high = [], []
    for f in range(FIELDS):
        sorted_side = jnp.dot(zface[f], order, preferred_element_type=f32)
        low.append(sorted_side[:, :nx])
        high.append(sorted_side[:, nx:])
    cells = jnp.concatenate(
        [jnp.concatenate(low, axis=1), jnp.concatenate(high, axis=1)], axis=0
    ).astype(bf16)
    own_rows = yface[...].astype(bf16)
    rows = blocks * send_ref.shape[1]
    slots = lax.broadcasted_iota(jnp.int32, (rows, 2 * nz + 2 * ny), 0)
    chosen = jnp.where(slots.astype(f32) == target, 1.0, 0.0).astype(bf16)
    packed = lax.dot_general(
        chosen[:, : 2 * nz],
        own_rows.reshape(FIELDS * nx, 2 * nz),
        (((1,), (1,)), ((), ())),
        preferred_element_type=f32,
    )
    packed = packed + jnp.dot(chosen[:, 2 * nz :], cells, preferred_element_type=f32)
    send_ref[...] = packed.astype(bf16).reshape(send_ref.shape)

    patches = [patch_copy(shift) for shift in range(1, blocks)]
    for copy in patches:
        copy.start()
    landed[me] = send_ref[me]

    corner_first = float(inverse[0, 0])
    corner_last = float(inverse[nx - 1, nx - 1])
    shared = 1.0 / (1.0 - lhs_alpha * lhs_alpha * corner_first * corner_last)

    @pl.when(has_left)
    def _():
        ends_right.wait_recv()

    @pl.when(has_right)
    def _():
        ends_left.wait_recv()

    for f in range(FIELDS):
        terms = halo_terms(f)
        before_last = beside[0, f].astype(f32)
        after_first = beside[1, f].astype(f32)
        left = (before_last - lhs_alpha * corner_last * ends[0, f]) * shared
        next_last = (ends[1, f] - lhs_alpha * corner_last * after_first) * shared
        right = after_first - lhs_alpha * corner_first * next_last
        edge_ref[f, 0] = terms[0] - jnp.where(has_left, lhs_alpha * left, 0.0)
        edge_ref[f, 1] = terms[1]
        edge_ref[f, 2] = terms[2]
        edge_ref[f, 3] = terms[3] - jnp.where(has_right, lhs_alpha * right, 0.0)

    for copy in patches:
        copy.wait_recv()
    received = landed[...].reshape(rows, FIELDS * nx)
    slots = lax.broadcasted_iota(jnp.int32, (rows, 2 * nz), 0)
    ypick = jnp.where(slots.astype(f32) == yorigin, 1.0, 0.0).astype(bf16)
    yother = lax.dot_general(
        received, ypick, (((0,), (0,)), ((), ())), preferred_element_type=f32
    ).reshape(FIELDS, nx, 2 * nz)
    ypen_ref[...] = ylive * (yother - yface[...])
    slots = lax.broadcasted_iota(jnp.int32, (2 * ny, rows), 1)
    zpick = jnp.where(slots.astype(f32) == zorigin, 1.0, 0.0).astype(bf16)
    zcells = jnp.dot(zpick, received, preferred_element_type=f32).astype(bf16)
    row = lax.broadcasted_iota(jnp.int32, (2 * nx, nz), 0)
    col = lax.broadcasted_iota(jnp.int32, (2 * nx, nz), 1)
    wanted = jnp.where(row < nx, 2 * row + 1, 2 * (row - nx))
    order = jnp.where(col == wanted, 1.0, 0.0).astype(bf16)
    zmask = jnp.where(lane % 2 == 1, zlive[:ny], zlive[ny:])
    for f in range(FIELDS):
        both = jnp.concatenate(
            [zcells[:ny, f * nx : (f + 1) * nx], zcells[ny:, f * nx : (f + 1) * nx]], axis=1
        )
        zother = jnp.dot(both, order, preferred_element_type=f32)
        zpen_ref[f] = zmask * (zother - zface[f].astype(f32))
    for copy in patches:
        copy.wait_send()

    @pl.when(has_right)
    def _():
        halo_right.wait_send()
        ends_right.wait_send()

    @pl.when(has_left)
    def _():
        halo_left.wait_send()
        ends_left.wait_send()


def main_kernel(
    nx, ny, nz, bx,
    upper_ref, adj_hbm, edge_ref, ypen, zpen,
    dy_ref, dz_ref, rho_ref, vel_ref, prs_ref, met_x_ref, met_y_ref, met_z_ref,
    out_ref,
    adj_ref, load_sem, sweep, carry, gyz,
):
    metric_refs = (met_x_ref, met_y_ref, met_z_ref)
    step = pl.program_id(0)
    block = pl.num_programs(0) - 1 - step
    weight, upper = sweep_coefs(nx)
    part = 32 if ny % 32 == 0 else ny

    @pl.when(step == 0)
    def _():
        half = nx // 2

        def load(f, h):
            at = pl.ds(h * half, half)
            return pltpu.make_async_copy(
                adj_hbm.at[f, at], adj_ref.at[f, at], load_sem.at[2 * f + h]
            )

        for f in range(FIELDS):
            for h in range(2):
                load(f, h).start()
        def forward(index, state):
            f = index // (ny // part)
            at = pl.ds(pl.multiple_of((index % (ny // part)) * part, part), part)

            @pl.when(index % (ny // part) == 0)
            def _():
                load(f, 0).wait()
                load(f, 1).wait()

            zero = jnp.zeros((part, nz), f32)
            window = [zero, zero, adj_ref[f, 0, at, :].astype(f32), adj_ref[f, 1, at, :].astype(f32)]
            before = zero
            for x in range(nx):
                ahead = adj_ref[f, x + 2, at, :].astype(f32) if x + 2 < nx else zero
                window.append(ahead)
                total = near_coef / far_coef * (window[3] - window[1]) + (window[4] - window[0])
                scale = float(weight[x])
                if x < 2 or x >= nx - 2:
                    total = far_coef * total + edge_ref[f, x if x < 2 else x - nx + 4, at, :]
                else:
                    scale = scale * far_coef
                before = scale * total - float(upper[x]) * before
                sweep[f, x, at, :] = before
                window = window[1:]
            return state

        lax.fori_loop(0, FIELDS * (ny // part), forward, 0)
        carry[...] = jnp.zeros_like(carry)

    chunk = 16 if ny % 16 == 0 else ny
    unroll = 4
    row = lax.broadcasted_iota(jnp.int32, (chunk, nz), 0)
    lane = lax.broadcasted_iota(jnp.int32, (chunk, nz), 1)
    zedge = (lane == 0) | (lane == nz - 1)

    def one(j, slot):
        x = block * bx + j
        slabs = [adj_ref[f, x] for f in range(FIELDS)]
        tall = jnp.concatenate(slabs, axis=0)
        gyz[slot, 0] = jnp.dot(
            jnp.concatenate([tall, tall], axis=1), dz_ref[...], preferred_element_type=f32
        ).reshape(FIELDS, ny, nz)
        wide = jnp.concatenate(slabs, axis=1)
        across = jnp.dot(
            dy_ref[...], jnp.concatenate([wide, wide], axis=0), preferred_element_type=f32
        )
        for f in range(FIELDS):
            gyz[slot, 1, f] = across[:, f * nz : (f + 1) * nz]
        back = upper_ref[x]
        group = pl.ds(pl.multiple_of(block * bx, bx), bx)
        for y0 in range(0, ny, chunk):
            at = slice(y0, y0 + chunk)
            gx = []
            for f in range(FIELDS):
                value = sweep[f, x, at, :] - back * carry[f, at, :]
                carry[f, at, :] = value
                gx.append(value)
            gy = [gyz[slot, 1, f, at, :] for f in range(FIELDS)]
            gz = [gyz[slot, 0, f, at, :] for f in range(FIELDS)]
            rho = rho_ref[j, at, :].astype(f32)
            vel = [vel_ref[c, j, at, :].astype(f32) for c in range(3)]
            prs = heat_ratio * prs_ref[j, at, :].astype(f32)
            totals = [None] * FIELDS

            def add(i, value):
                totals[i] = value if totals[i] is None else totals[i] + value

            turned = None
            for d, g in enumerate((gx, gy, gz)):
                k = [metric_refs[d][c, j, at, :].astype(f32) for c in range(3)]
                speed = k[0] * vel[0] + k[1] * vel[1] + k[2] * vel[2]
                coupled = rho * g[0] + prs * g[4]
                for i in range(FIELDS):
                    add(i, speed * g[i])
                for i in range(3):
                    add(i + 1, k[i] * coupled)
                dot = k[0] * g[1] + k[1] * g[2] + k[2] * g[3]
                turned = dot if turned is None else turned + dot
            inverse = pl.reciprocal(rho, approx=True)
            inverse = inverse * (2.0 - rho * inverse)
            add(4, turned * inverse)
            for f in range(FIELDS):
                jump = pltpu.roll(zpen[f, at, :], nz - 1 - 2 * x, 1)
                total = totals[f] + jnp.where(zedge, jump, 0.0)
                if y0 == 0:
                    jump = pltpu.roll(ypen[f, group, 0:nz], lax.rem(bx - j, bx), 0)
                    jump = jnp.concatenate([jump] * (chunk // bx), axis=0)
                    total = total + jnp.where(row == 0, jump, 0.0)
                if y0 + chunk == ny:
                    jump = pltpu.roll(ypen[f, group, nz : 2 * nz], bx - 1 - j, 0)
                    jump = jnp.concatenate([jump] * (chunk // bx), axis=0)
                    total = total + jnp.where(row == chunk - 1, jump, 0.0)
                out_ref[f, j, at, :] = total.astype(bf16)

    def several(i, state):
        for u in range(unroll):
            one(bx - 1 - (i * unroll + u), u)
        return state

    lax.fori_loop(0, bx // unroll, several, 0)


def body(adjoint, density, velocity, pressure, metrics, links):
    adj = adjoint[:, 0]
    _, nx, ny, nz = adj.shape
    blocks, patches = links.shape[1:]
    blk_count = lax.axis_size("blk")
    segments = lax.axis_size("ax")
    capacity = -(-patches // blocks)
    inverse, derivative = tables(nx)

    slab = (capacity * PW, FIELDS * nx)
    layers = (FIELDS, 2, ny, nz)
    level = (FIELDS, ny, nz)
    vmem = pl.BlockSpec(memory_space=pltpu.VMEM)
    edges, ypen, zpen = pl.pallas_call(
        functools.partial(
            exchange_kernel, nx, ny, nz, blk_count, segments, inverse, derivative[[0, nx - 1]]
        ),
        out_shape=(
            jax.ShapeDtypeStruct((FIELDS, 4, ny, nz), f32),
            jax.ShapeDtypeStruct((FIELDS, nx, 2 * nz), f32),
            jax.ShapeDtypeStruct((FIELDS, ny, nz), f32),
        ),
        in_specs=[vmem, pl.BlockSpec(memory_space=pl.ANY)],
        out_specs=(vmem, vmem, vmem),
        scratch_shapes=[
            pltpu.VMEM((FIELDS, nx, ny, nz), bf16),
            pltpu.VMEM((blk_count,) + slab, bf16),
            pltpu.VMEM((FIELDS, nx, 2 * nz), f32),
            pltpu.VMEM(level, bf16),
            pltpu.VMEM((blk_count,) + slab, bf16),
            pltpu.VMEM((2,) + layers, bf16),
            pltpu.VMEM((2,) + level, f32),
            pltpu.VMEM((2,) + level, bf16),
            pltpu.VMEM((2,) + level, bf16),
            pltpu.SemaphoreType.DMA((FIELDS,)),
            pltpu.SemaphoreType.DMA((blk_count,)),
            pltpu.SemaphoreType.DMA((blk_count,)),
            pltpu.SemaphoreType.DMA((4,)),
            pltpu.SemaphoreType.DMA((4,)),
        ],
        compiler_params=pltpu.CompilerParams(
            collective_id=0, has_side_effects=True, vmem_limit_bytes=48 << 20
        ),
        name="exchange",
    )(links, adj)

    dy_high, dy_low = split(tables(ny)[1])
    dz_high, dz_low = split(tables(nz)[1])
    dy_both = jnp.asarray(np.concatenate([dy_high, dy_low], axis=1))
    dz_both = jnp.asarray(np.concatenate([dz_high.T, dz_low.T], axis=0))
    upper = jnp.asarray(sweep_coefs(nx)[1].astype(np.float32))

    bx = 8
    steps = nx // bx

    def whole(*shape):
        zeros = (0,) * len(shape)
        return pl.BlockSpec(shape, lambda i: zeros, pipeline_mode=pl.Buffered(1))

    def metric(d):
        return pl.BlockSpec((3, bx, ny, nz), lambda i: (d, steps - 1 - i, 0, 0))

    result = pl.pallas_call(
        functools.partial(main_kernel, nx, ny, nz, bx),
        grid=(steps,),
        out_shape=jax.ShapeDtypeStruct((FIELDS, nx, ny, nz), bf16),
        in_specs=[
            pl.BlockSpec(memory_space=pltpu.SMEM),
            pl.BlockSpec(memory_space=pl.ANY),
            whole(FIELDS, 4, ny, nz),
            whole(FIELDS, nx, 2 * nz),
            whole(FIELDS, ny, nz),
            whole(ny, 2 * ny),
            whole(2 * nz, nz),
            pl.BlockSpec((bx, ny, nz), lambda i: (steps - 1 - i, 0, 0)),
            pl.BlockSpec((3, bx, ny, nz), lambda i: (0, steps - 1 - i, 0, 0)),
            pl.BlockSpec((bx, ny, nz), lambda i: (steps - 1 - i, 0, 0)),
            metric(0),
            metric(1),
            metric(2),
        ],
        out_specs=pl.BlockSpec((FIELDS, bx, ny, nz), lambda i: (0, steps - 1 - i, 0, 0)),
        scratch_shapes=[
            pltpu.VMEM((FIELDS, nx, ny, nz), bf16),
            pltpu.SemaphoreType.DMA((2 * FIELDS,)),
            pltpu.VMEM((FIELDS, nx, ny, nz), f32),
            pltpu.VMEM((FIELDS, ny, nz), f32),
            pltpu.VMEM((4, 2, FIELDS, ny, nz), f32),
        ],
        compiler_params=pltpu.CompilerParams(vmem_limit_bytes=48 << 20),
        name="flux_and_penalty",
    )(
        upper, adj, edges, ypen, zpen, dy_both, dz_both,
        density[0], velocity[:, 0], pressure[0],
        metrics[:, 0], metrics[:, 0], metrics[:, 0],
    )
    return result[:, None]


def solution(mesh):
    in_specs = (
        P(None, "blk", "ax", None, None),
        P("blk", "ax", None, None),
        P(None, "blk", "ax", None, None),
        P("blk", "ax", None, None),
        P(None, "blk", "ax", None, None),
        P(),
    )
    out_specs = P(None, "blk", "ax", None, None)
    return jax.shard_map(body, mesh=mesh, in_specs=in_specs, out_specs=out_specs, check_vma=False)
```
